32 devices in a mesh: pipe: 4 (over y, core), expert: 4 (over z), dp: 2 (over x).
Axes of the slice: x: 2, y: 2, z: 4, core: 2. Of those that a mesh axis runs over, the one named last changes fastest.
Arguments:
- normed: bfloat16 [4, 4, 384, 4096], P('pipe', None, ('expert', 'dp')), may hold values from -1.5 to 1.5
- saved_out: bfloat16 [4, 4, 384, 2, 4096], P('pipe', None, ('expert', 'dp')), may hold values from -0.59765625 to 0.59765625
- expert_grads: bfloat16 [4, 4, 2, 4, 4, 36, 4096], P('pipe', None, 'dp', 'expert'), may hold values from -24 to 24
- routes: int32 [4, 4, 384, 2], P('pipe', None, ('expert', 'dp')), may hold values from 0 to 3, all different within a row; in each aligned block of 48 rows (0 to 47, 48 to 95, ..., all dimensions but the last counted through in order) at most 36 rows name the same one
- router_weight: bfloat16 [4, 4096, 4], P('pipe'), may hold values from -0.375 to 0.375
- upstream: bfloat16 [4, 384, 4096], P(None, ('expert', 'dp')), may hold values from -6 to 6
Outputs:
- grad_input: bfloat16 [4, 4, 384, 4096], P('pipe', None, ('expert', 'dp'))
- router_grad: float32 [4, 4096, 4], P('pipe')
The draws below stay inside these ranges and needn't reach their ends.
Inputs may be any that keep to these rules, and one draw needn't show every extreme that they name: `routes`: the two experts of a row differ. Within the 48 rows of one device for one section and micro-batch no expert is named more than 36 times, a bound that some expert reaches in some of these blocks.
All inputs are finite; a program needn't handle non-finite values.
Results may differ from the reference program's by a relative error of at most 0.007.
Values may be sent and summed in bfloat16 or wider, within the bound.
A program may use at most 128 MiB of HBM per device.

```python
import math
import jax
import jax.numpy as jnp
import numpy as np

D = 4096
TOP = 2
MICRO = 4
ROWS = 48
EXPERTS = 4
CAP = 36
TOK_MB = 384
N_PIPE = 4
N_EXPERT = 4
N_DP = 2


def level_of(key, shape, split, least, high):
    def one(dim, blocks):
        steps = jax.random.uniform(jax.random.fold_in(jax.random.fold_in(key, 6), dim), (blocks,), jnp.float32, least / len(split), high / len(split))
        return jnp.repeat(jnp.exp(steps), shape[dim] // blocks).reshape((-1,) + (1,) * (len(shape) - dim - 1))

    gain = one(*split[0])
    for cut in split[1:]:
        gain = gain * one(*cut)
    return gain


def shared_out(stream_key, own, number, rows, count, top, reach, skew):
    order = jax.random.permutation(stream_key, count)
    heavy_load, ordinary = shares(count, rows * top, reach, skew, True), shares(count, rows * top, reach, skew, False)
    places = jnp.arange(count)

    def named(tallies, turn):
        used = int((tallies > 0).sum())
        fixed = max(1, used // 4)
        shifted = fixed + (places - fixed + turn * (used - fixed)) % max(1, count - fixed)
        return jnp.zeros((count,), jnp.int32).at[order[jnp.where(places < fixed, places, shifted)]].set(jnp.asarray(tallies, jnp.int32))

    tallies = jnp.where(number % 4 == 0, named(heavy_load, number // 4), named(ordinary, number - number // 4 - 1))
    mixed = jax.random.permutation(jax.random.fold_in(own, 3), count)
    source_of, sink = mixed[0:count // 2 * 2:2], mixed[1:count // 2 * 2:2]
    margin = jnp.minimum(tallies[source_of] - 1, reach - tallies[sink]) // 2
    margin = jnp.where((source_of == order[0]) | (sink == order[0]) | (tallies[sink] == 0), 0, jnp.maximum(margin, 0))
    shifted = jax.random.randint(jax.random.fold_in(own, 4), (count // 2,), 0, 1 << 20) % (margin + 1)
    tallies = tallies.at[source_of].add(-shifted).at[sink].add(shifted)
    labels = jnp.searchsorted(jnp.cumsum(tallies), jnp.arange(rows * top), side="right").astype(jnp.int32)
    listing = labels.reshape(top, rows).T
    listing = listing[jax.random.permutation(jax.random.fold_in(own, 1), rows)]
    turn = jax.random.randint(jax.random.fold_in(own, 2), (rows, 1), 0, top)
    return jnp.take_along_axis(listing, (jnp.arange(top)[None, :] + turn) % top, axis=1)


def shares(count, total, limit, slope, full):
    portions = [(1 << 20) // math.isqrt(rank ** slope) + 1 for rank in range(1, count + 1)]
    largest = limit if full else min(limit, max(-(-total // count), total * portions[0] // sum(portions)))
    least = 1 if total - largest >= count - 1 else 0
    counts, surplus = [largest] + [least] * (count - 1), total - largest - least * (count - 1)
    while surplus > 0:
        free = [i for i in range(1, count) if counts[i] < largest] or [i for i in range(1, count) if counts[i] < limit]
        whole, budget = sum([portions[i] for i in free]), surplus
        for i in free:
            more = min(limit - counts[i], max(1, budget * portions[i] // whole), surplus)
            counts[i] = counts[i] + more
            surplus = surplus - more
    return np.array(counts)


def gaussian(rng, shape, deviation, reach, split=(), kind=jnp.bfloat16):
    array = jax.random.normal(rng, shape, jnp.float32) * deviation
    if len(split) > 0:
        array = level_of(rng, shape, split, -0.22, 0.18) * array
    return jnp.clip(array, min=-reach, max=reach).astype(kind)


def setup_inputs(seed: int = 0) -> dict:
    keys = jax.random.split(jax.random.key(seed), 7)
    normed = gaussian(keys[0], (N_PIPE, MICRO, TOK_MB, D), 0.25, 1.5, ((0, 4), (2, 8)))
    saved_out = gaussian(keys[1], (N_PIPE, MICRO, TOK_MB, TOP, D), 0.1, 0.59765625, ((0, 4), (2, 8)))
    expert_grads = gaussian(keys[2], (N_PIPE, MICRO, N_DP, EXPERTS, N_EXPERT, CAP, D), 4.0, 24.0, ((0, 4), (2, 2), (3, 4)))
    routes_keys = jax.random.split(jax.random.fold_in(keys[3], 1), N_PIPE * MICRO * TOK_MB // ROWS)
    routes_turns = jax.random.permutation(jax.random.fold_in(keys[3], 3), N_PIPE * MICRO * TOK_MB // ROWS)
    routes = jax.vmap(lambda own, number: shared_out(jax.random.fold_in(keys[3], 2), own, number, ROWS, EXPERTS, TOP, CAP, 2))(routes_keys, routes_turns).reshape((N_PIPE, MICRO, TOK_MB, TOP))
    router_weight = gaussian(keys[4], (N_PIPE, D, EXPERTS), (D // 16) ** -0.5, 0.375, ((0, 4),))
    upstream = gaussian(keys[5], (MICRO, TOK_MB, D), 1.0, 6.0, ((1, 8),))
    return {"normed": normed, "saved_out": saved_out, "expert_grads": expert_grads, "routes": routes, "router_weight": router_weight, "upstream": upstream}


def slot_index(flat, experts, capacity):
    onehot = (flat[..., None] == jnp.arange(experts, dtype=jnp.int32)).astype(jnp.int32)
    before = jnp.cumsum(onehot, axis=-2) - onehot
    position = jnp.sum(before * onehot, axis=-1).astype(jnp.int32)
    return (flat * capacity + position).astype(jnp.int32)


def take_rows(buffer, index):
    return buffer[index]


def reference(normed, saved_out, expert_grads, routes, router_weight, upstream):
    groups = N_EXPERT * N_DP
    grads = [None] * N_PIPE
    weight_grads = [None] * N_PIPE
    incoming = upstream
    for section_num in reversed(range(N_PIPE)):
        buffer = jnp.transpose(expert_grads[section_num], (0, 3, 1, 2, 4, 5)).reshape(MICRO, groups, EXPERTS * CAP, D)
        flat = routes[section_num].reshape(MICRO, groups, ROWS * TOP)
        index = slot_index(flat, EXPERTS, CAP)
        back = jax.vmap(jax.vmap(take_rows))(buffer, index).reshape(MICRO, TOK_MB, TOP, D).astype(jnp.float32)
        router_w = router_weight[section_num]
        rows_2d = normed[section_num].reshape(MICRO * TOK_MB, D)
        logits = jnp.dot(rows_2d, router_w, preferred_element_type=jnp.float32).reshape(MICRO, TOK_MB, EXPERTS)
        expl = jnp.exp(logits)
        probs = expl / jnp.sum(expl, axis=-1, keepdims=True)
        chosen = (routes[section_num][..., None] == jnp.arange(EXPERTS, dtype=jnp.int32)).astype(jnp.float32)
        gates = jnp.einsum("mtke,mte->mtk", chosen, probs)
        dot_grads = jnp.einsum("mtd,mtkd->mtk", incoming.astype(jnp.float32), saved_out[section_num].astype(jnp.float32))
        weighted = dot_grads * gates
        dense_f = jnp.einsum("mtke,mtk->mte", chosen, weighted) - probs * jnp.sum(weighted, axis=-1)[..., None]
        dense = dense_f.astype(jnp.bfloat16)
        dense_2d = dense.reshape(MICRO * TOK_MB, EXPERTS)
        router_term = jnp.dot(dense_2d, router_w.T, preferred_element_type=jnp.float32).reshape(MICRO, TOK_MB, D)
        total = incoming.astype(jnp.float32) + gates[..., 0, None] * back[:, :, 0] + gates[..., 1, None] * back[:, :, 1] + router_term
        new_grad = total.astype(jnp.bfloat16)
        weight_grads[section_num] = jnp.dot(rows_2d.T, dense_2d, preferred_element_type=jnp.float32) / MICRO
        grads[section_num] = new_grad
        incoming = new_grad
    return jnp.stack(grads), jnp.stack(weight_grads)
```

```python
import functools

import jax
import jax.numpy as jnp
from jax import lax
from jax.experimental import pallas as pl
from jax.experimental.pallas import tpu as pltpu
from jax.sharding import PartitionSpec as P

MESH = pl.DeviceIdType.MESH
PACK = 16


def kernel(
    sizes,
    grads_ref,
    tail_ref,
    normed_ref,
    saved_ref,
    upstream_ref,
    routes_ref,
    weight_ref,
    out_ref,
    wgrad_ref,
    main_v,
    tail_v,
    normed_v,
    saved_v,
    inc_v,
    total_v,
    pick_v,
    probs_v,
    chosen_v,
    wpart_v,
    wrecv_v,
    main_send,
    main_recv,
    tail_send,
    tail_recv,
    main_own,
    tail_own,
    load_sem,
    top_sem,
    relay_send,
    relay_recv,
    part_send,
    part_recv,
    sum_send,
    sum_recv,
):
    n_pipe, n_expert, n_dp = sizes
    micro, rows, width = normed_v.shape
    experts = weight_ref.shape[0]
    capacity = grads_ref.shape[2]
    whole_rows = capacity // PACK * PACK
    rest = capacity - whole_rows
    tail_rows = tail_v.shape[1]
    group = n_expert * n_dp
    chunks, _, chunk = wpart_v.shape
    tile = min(width, 512)
    pipe = lax.axis_index("pipe")
    expert = lax.axis_index("expert")
    dp = lax.axis_index("dp")
    me = expert * n_dp + dp

    def member(distance):
        other = lax.rem(me + distance, group)
        return other, {"expert": other // n_dp, "dp": lax.rem(other, n_dp)}

    barrier = pltpu.get_barrier_semaphore()
    for distance in range(1, group):
        _, place = member(distance)
        pl.semaphore_signal(barrier, inc=1, device_id=place, device_id_type=MESH)

    @pl.when(pipe > 0)
    def _():
        pl.semaphore_signal(barrier, inc=1, device_id={"pipe": pipe - 1}, device_id_type=MESH)

    @pl.when(pipe < n_pipe - 1)
    def _():
        pl.semaphore_signal(barrier, inc=1, device_id={"pipe": pipe + 1}, device_id_type=MESH)

    loads = [
        pltpu.make_async_copy(normed_ref, normed_v, load_sem.at[0]),
        pltpu.make_async_copy(saved_ref, saved_v, load_sem.at[1]),
    ]
    top_load = pltpu.make_async_copy(upstream_ref, inc_v, top_sem)
    for load in loads:
        load.start()

    @pl.when(pipe == n_pipe - 1)
    def _():
        top_load.start()

    pl.semaphore_wait(
        barrier,
        group - 1 + jnp.where(pipe > 0, 1, 0) + jnp.where(pipe < n_pipe - 1, 1, 0),
    )

    def tail_copy(distance):
        other = lax.rem(expert + distance, n_expert)
        return pltpu.make_async_remote_copy(
            src_ref=tail_ref.at[other],
            dst_ref=tail_v.at[expert],
            send_sem=tail_send.at[other],
            recv_sem=tail_recv.at[expert],
            device_id={"expert": other},
            device_id_type=MESH,
        )

    def main_copy(m, distance):
        other = lax.rem(expert + distance, n_expert)
        return pltpu.make_async_remote_copy(
            src_ref=grads_ref.at[m, other, pl.ds(0, whole_rows)],
            dst_ref=main_v.at[m, expert],
            send_sem=main_send.at[m, other],
            recv_sem=main_recv.at[m, expert],
            device_id={"expert": other},
            device_id_type=MESH,
        )

    def tail_arrival(distance):
        other = lax.rem(expert + distance, n_expert)
        return pltpu.make_async_remote_copy(
            src_ref=tail_ref.at[other],
            dst_ref=tail_v.at[other],
            send_sem=tail_send.at[other],
            recv_sem=tail_recv.at[other],
            device_id={"expert": other},
            device_id_type=MESH,
        )

    def main_arrival(m, distance):
        other = lax.rem(expert + distance, n_expert)
        return pltpu.make_async_remote_copy(
            src_ref=grads_ref.at[m, other, pl.ds(0, whole_rows)],
            dst_ref=main_v.at[m, other],
            send_sem=main_send.at[m, other],
            recv_sem=main_recv.at[m, other],
            device_id={"expert": other},
            device_id_type=MESH,
        )

    def own_main(m):
        return pltpu.make_async_copy(
            grads_ref.at[m, expert, pl.ds(0, whole_rows)], main_v.at[m, expert], main_own.at[m]
        )

    own_tail = pltpu.make_async_copy(tail_ref.at[expert], tail_v.at[expert], tail_own)

    if rest:
        for distance in range(1, n_expert):
            tail_copy(distance).start()
        own_tail.start()
    if whole_rows:
        for m in range(micro):
            for distance in range(1, n_expert):
                main_copy(m, distance).start()
            own_main(m).start()

    wpart_v[...] = jnp.zeros_like(wpart_v)
    for load in loads:
        load.wait()

    weight = weight_ref[...]
    earlier = (
        lax.broadcasted_iota(jnp.int32, (rows, rows), 0)
        > lax.broadcasted_iota(jnp.int32, (rows, rows), 1)
    ).astype(jnp.bfloat16)
    expert_ids = lax.broadcasted_iota(jnp.int32, (rows, experts), 1)

    def route(m, carry):
        logits = lax.dot_general(
            normed_v[m], weight, (((1,), (1,)), ((), ())), preferred_element_type=jnp.float32
        )
        expl = jnp.exp(logits)
        probs = expl / jnp.sum(expl, axis=-1, keepdims=True)
        probs_v[m] = probs
        named = routes_ref[m]
        first = (named[:, 0:1] == expert_ids).astype(jnp.float32)
        second = (named[:, 1:2] == expert_ids).astype(jnp.float32)
        chosen_v[m, 0] = first
        chosen_v[m, 1] = second
        either = first + second
        before = jnp.dot(earlier, either.astype(jnp.bfloat16), preferred_element_type=jnp.float32)
        slot = jnp.where(either > 0.5, before.astype(jnp.int32), -1)
        parts = []
        if whole_rows:
            ids = lax.broadcasted_iota(jnp.int32, (rows, whole_rows), 1)
            for e in range(experts):
                parts.append(jnp.where(slot[:, e : e + 1] == ids, probs[:, e : e + 1], 0.0))
        if rest:
            ids = lax.broadcasted_iota(jnp.int32, (rows, tail_rows), 1)
            for e in range(experts):
                at = slot[:, e : e + 1]
                there = jnp.where(at >= whole_rows, at - whole_rows + m * rest, -1)
                parts.append(jnp.where(there == ids, probs[:, e : e + 1], 0.0))
        pick = jnp.concatenate(parts, axis=1)
        high = pick.astype(jnp.bfloat16)
        low = (pick - high.astype(jnp.float32)).astype(jnp.bfloat16)
        pick_v[m, pl.ds(0, rows)] = high
        pick_v[m, pl.ds(rows, rows)] = low
        return carry

    lax.fori_loop(0, micro, route, 0)

    if rest:
        for distance in range(1, n_expert):
            tail_arrival(distance).wait_recv()
        own_tail.wait()

    @pl.when(pipe == n_pipe - 1)
    def _():
        top_load.wait()

    main_columns = experts * whole_rows
    pair = lax.broadcasted_iota(jnp.int32, (rows, 2 * rows), 1) - 2 * lax.broadcasted_iota(
        jnp.int32, (rows, 2 * rows), 0
    )

    def relay(m):
        return pltpu.make_async_remote_copy(
            src_ref=out_ref.at[m],
            dst_ref=inc_v.at[m],
            send_sem=relay_send.at[m],
            recv_sem=relay_recv.at[m],
            device_id={"pipe": jnp.maximum(pipe - 1, 0)},
            device_id_type=MESH,
        )

    def block(m, carry):
        if whole_rows:
            for distance in range(1, n_expert):
                main_arrival(m, distance).wait_recv()
            own_main(m).wait()
        pick = pick_v[m]

        def combine(i, inner):
            cols = pl.ds(pl.multiple_of(i * tile, tile), tile)
            both = jnp.zeros((2 * rows, tile), jnp.float32)
            if whole_rows:
                both += jnp.dot(
                    pick[:, :main_columns],
                    main_v[m, :, :, cols].reshape(main_columns, tile),
                    preferred_element_type=jnp.float32,
                )
            if rest:
                both += jnp.dot(
                    pick[:, main_columns:],
                    tail_v[:, :, cols].reshape(experts * tail_rows, tile),
                    preferred_element_type=jnp.float32,
                )
            total_v[:, cols] = both[:rows] + both[rows:]
            return inner

        lax.fori_loop(0, width // tile, combine, 0)

        @pl.when(pipe < n_pipe - 1)
        def _():
            relay(m).wait_recv()

        cross = lax.dot_general(
            inc_v[m], saved_v[m], (((1,), (1,)), ((), ())), preferred_element_type=jnp.float32
        )
        probs = probs_v[m]
        weighted = jnp.zeros((rows, experts), jnp.float32)
        for k in range(2):
            dot = jnp.sum(jnp.where(pair == k, cross, 0.0), axis=1, keepdims=True)
            weighted += dot * probs * chosen_v[m, k]
        dense = (weighted - probs * jnp.sum(weighted, axis=1, keepdims=True)).astype(jnp.bfloat16)

        def finish(i, inner):
            cols = pl.ds(pl.multiple_of(i * tile, tile), tile)
            term = jnp.dot(dense, weight_ref[:, cols], preferred_element_type=jnp.float32)
            whole = inc_v[m, :, cols].astype(jnp.float32) + total_v[:, cols] + term
            out_ref[m, :, cols] = whole.astype(jnp.bfloat16)
            return inner

        lax.fori_loop(0, width // tile, finish, 0)

        @pl.when(pipe > 0)
        def _():
            relay(m).start()

        def weigh(i, inner):
            cols = pl.ds(pl.multiple_of(i * chunk, chunk), chunk)
            wpart_v[i] += lax.dot_general(
                dense,
                normed_v[m, :, cols],
                (((0,), (0,)), ((), ())),
                preferred_element_type=jnp.float32,
            )
            return inner

        lax.fori_loop(0, chunks, weigh, 0)
        return carry

    lax.fori_loop(0, micro, block, 0)

    def part_copy(distance):
        other, place = member(distance)
        return pltpu.make_async_remote_copy(
            src_ref=wpart_v.at[jnp.minimum(other, chunks - 1)],
            dst_ref=wrecv_v.at[me],
            send_sem=part_send.at[other],
            recv_sem=part_recv.at[me],
            device_id=place,
            device_id_type=MESH,
        ), other

    def part_arrival(distance):
        other, place = member(distance)
        return pltpu.make_async_remote_copy(
            src_ref=wpart_v.at[0],
            dst_ref=wrecv_v.at[other],
            send_sem=part_send.at[other],
            recv_sem=part_recv.at[other],
            device_id=place,
            device_id_type=MESH,
        )

    def sum_copy(distance):
        other, place = member(distance)
        spot = jnp.minimum(me, chunks - 1)
        return pltpu.make_async_remote_copy(
            src_ref=wgrad_ref.at[spot],
            dst_ref=wgrad_ref.at[spot],
            send_sem=sum_send.at[other],
            recv_sem=sum_recv.at[me],
            device_id=place,
            device_id_type=MESH,
        )

    def sum_arrival(distance):
        other, place = member(distance)
        spot = jnp.minimum(other, chunks - 1)
        return pltpu.make_async_remote_copy(
            src_ref=wgrad_ref.at[spot],
            dst_ref=wgrad_ref.at[spot],
            send_sem=sum_send.at[other],
            recv_sem=sum_recv.at[other],
            device_id=place,
            device_id_type=MESH,
        ), other

    for distance in range(1, group):
        copy, other = part_copy(distance)

        @pl.when(other < chunks)
        def _():
            copy.start()

    @pl.when(me < chunks)
    def _():
        total = wpart_v[me]
        for distance in range(1, group):
            part_arrival(distance).wait_recv()
            total += wrecv_v[member(distance)[0]]
        wgrad_ref[me] = total * (1.0 / micro)
        for distance in range(1, group):
            sum_copy(distance).start()

    for distance in range(1, group):
        copy, other = sum_arrival(distance)

        @pl.when(other < chunks)
        def _():
            copy.wait_recv()

    if rest:
        for distance in range(1, n_expert):
            tail_copy(distance).wait_send()
    if whole_rows:
        for m in range(micro):
            for distance in range(1, n_expert):
                main_copy(m, distance).wait_send()

    @pl.when(pipe > 0)
    def _():
        for m in range(micro):
            relay(m).wait_send()

    for distance in range(1, group):
        copy, other = part_copy(distance)

        @pl.when(other < chunks)
        def _():
            copy.wait_send()

    @pl.when(me < chunks)
    def _():
        for distance in range(1, group):
            sum_copy(distance).wait_send()


def on_device(sizes, normed, saved_out, expert_grads, routes, router_weight, upstream):
    n_pipe, n_expert, n_dp = sizes
    micro, rows, width = normed.shape[1:]
    experts = router_weight.shape[2]
    capacity = expert_grads.shape[5]
    whole_rows = capacity // PACK * PACK
    rest = capacity - whole_rows
    tail_rows = -(-max(rest * micro, 1) // PACK) * PACK
    group = n_expert * n_dp
    chunks = min(group, width // 128)
    chunk = width // chunks
    grads = expert_grads.reshape(micro, n_expert, capacity, width)
    tail = jnp.transpose(grads[:, :, whole_rows:], (1, 0, 2, 3)).reshape(n_expert, rest * micro, width)
    tail = jnp.pad(tail, ((0, 0), (0, tail_rows - rest * micro), (0, 0)))
    columns = experts * (whole_rows + (tail_rows if rest else 0))
    any_space = pl.BlockSpec(memory_space=pl.ANY)
    vmem = pl.BlockSpec(memory_space=pltpu.VMEM)
    dma = pltpu.SemaphoreType.DMA
    out, wgrad = pl.pallas_call(
        functools.partial(kernel, sizes),
        out_shape=(
            jax.ShapeDtypeStruct((micro, rows, width), jnp.bfloat16),
            jax.ShapeDtypeStruct((chunks, experts, chunk), jnp.float32),
        ),
        in_specs=[any_space] * 5 + [vmem] * 2,
        out_specs=(vmem, vmem),
        scratch_shapes=[
            pltpu.VMEM((micro, n_expert, max(whole_rows, PACK), width), jnp.bfloat16),
            pltpu.VMEM((n_expert, tail_rows, width), jnp.bfloat16),
            pltpu.VMEM((micro, rows, width), jnp.bfloat16),
            pltpu.VMEM((micro, 2 * rows, width), jnp.bfloat16),
            pltpu.VMEM((micro, rows, width), jnp.bfloat16),
            pltpu.VMEM((rows, width), jnp.float32),
            pltpu.VMEM((micro, 2 * rows, columns), jnp.bfloat16),
            pltpu.VMEM((micro, rows, experts), jnp.float32),
            pltpu.VMEM((micro, 2, rows, experts), jnp.float32),
            pltpu.VMEM((chunks, experts, chunk), jnp.float32),
            pltpu.VMEM((group, experts, chunk), jnp.float32),
            dma((micro, n_expert)),
            dma((micro, n_expert)),
            dma((n_expert,)),
            dma((n_expert,)),
            dma((micro,)),
            dma,
            dma((2,)),
            dma,
            dma((micro,)),
            dma((micro,)),
            dma((group,)),
            dma((group,)),
            dma((group,)),
            dma((group,)),
        ],
        compiler_params=pltpu.CompilerParams(
            collective_id=0, has_side_effects=True, vmem_limit_bytes=48 * 2**20
        ),
        name="relay",
    )(
        grads,
        tail,
        normed[0],
        saved_out.reshape(micro, 2 * rows, width),
        upstream,
        routes[0],
        router_weight[0].T,
    )
    router_grad = jnp.transpose(wgrad, (0, 2, 1)).reshape(width, experts)
    return (out[None], router_grad[None])


def solution(mesh):
    in_specs = (
        P("pipe", None, ("expert", "dp"), None),
        P("pipe", None, ("expert", "dp"), None, None),
        P("pipe", None, "dp", "expert", None, None, None),
        P("pipe", None, ("expert", "dp"), None),
        P("pipe", None, None),
        P(None, ("expert", "dp"), None),
    )
    out_specs = (P("pipe", None, ("expert", "dp"), None), P("pipe", None, None))
    sizes = (mesh.shape["pipe"], mesh.shape["expert"], mesh.shape["dp"])
    return jax.shard_map(
        functools.partial(on_device, sizes),
        mesh=mesh,
        in_specs=in_specs,
        out_specs=out_specs,
        check_vma=False,
    )
```

```python
import functools

import jax
import jax.numpy as jnp
from jax import lax
from jax.experimental import pallas as pl
from jax.experimental.pallas import tpu as pltpu
from jax.sharding import PartitionSpec as P

MESH = pl.DeviceIdType.MESH
PACK = 16


def kernel(
    sizes,
    grads_ref,
    tail_ref,
    normed_ref,
    saved_ref,
    upstream_ref,
    routes_ref,
    weight_ref,
    out_ref,
    wgrad_ref,
    main_v,
    tail_v,
    normed_v,
    pairs_v,
    saved_v,
    inc_v,
    total_v,
    dense_v,
    pick_v,
    probs_v,
    chosen_v,
    wpart_v,
    wrecv_v,
    main_send,
    main_recv,
    tail_send,
    tail_recv,
    main_own,
    tail_own,
    load_sem,
    top_sem,
    relay_send,
    relay_recv,
    part_send,
    part_recv,
    sum_send,
    sum_recv,
):
    n_pipe, n_expert, n_dp = sizes
    micro, rows, width = normed_v.shape
    experts = weight_ref.shape[0]
    capacity = grads_ref.shape[2]
    whole_rows = capacity // PACK * PACK
    rest = capacity - whole_rows
    tail_rows = tail_v.shape[1]
    group = n_expert * n_dp
    chunks, _, chunk = wpart_v.shape
    tile = min(width, 512)
    pipe = lax.axis_index("pipe")
    expert = lax.axis_index("expert")
    dp = lax.axis_index("dp")
    me = expert * n_dp + dp

    def member(distance):
        other = lax.rem(me + distance, group)
        return other, {"expert": other // n_dp, "dp": lax.rem(other, n_dp)}

    barrier = pltpu.get_barrier_semaphore()
    for distance in range(1, group):
        _, place = member(distance)
        pl.semaphore_signal(barrier, inc=1, device_id=place, device_id_type=MESH)

    @pl.when(pipe > 0)
    def _():
        pl.semaphore_signal(barrier, inc=1, device_id={"pipe": pipe - 1}, device_id_type=MESH)

    @pl.when(pipe < n_pipe - 1)
    def _():
        pl.semaphore_signal(barrier, inc=1, device_id={"pipe": pipe + 1}, device_id_type=MESH)

    loads = [
        pltpu.make_async_copy(normed_ref, normed_v, load_sem.at[0]),
        pltpu.make_async_copy(saved_ref, pairs_v, load_sem.at[1]),
    ]
    top_load = pltpu.make_async_copy(upstream_ref, inc_v, top_sem)
    for load in loads:
        load.start()

    @pl.when(pipe == n_pipe - 1)
    def _():
        top_load.start()

    pl.semaphore_wait(
        barrier,
        group - 1 + jnp.where(pipe > 0, 1, 0) + jnp.where(pipe < n_pipe - 1, 1, 0),
    )

    def tail_copy(distance):
        other = lax.rem(expert + distance, n_expert)
        return pltpu.make_async_remote_copy(
            src_ref=tail_ref.at[other],
            dst_ref=tail_v.at[expert],
            send_sem=tail_send.at[other],
            recv_sem=tail_recv.at[expert],
            device_id={"expert": other},
            device_id_type=MESH,
        )

    def main_copy(m, distance):
        other = lax.rem(expert + distance, n_expert)
        return pltpu.make_async_remote_copy(
            src_ref=grads_ref.at[m, other, pl.ds(0, whole_rows)],
            dst_ref=main_v.at[m, expert],
            send_sem=main_send.at[m, other],
            recv_sem=main_recv.at[m, expert],
            device_id={"expert": other},
            device_id_type=MESH,
        )

    def tail_arrival(distance):
        other = lax.rem(expert + distance, n_expert)
        return pltpu.make_async_remote_copy(
            src_ref=tail_ref.at[other],
            dst_ref=tail_v.at[other],
            send_sem=tail_send.at[other],
            recv_sem=tail_recv.at[other],
            device_id={"expert": other},
            device_id_type=MESH,
        )

    def main_arrival(m, distance):
        other = lax.rem(expert + distance, n_expert)
        return pltpu.make_async_remote_copy(
            src_ref=grads_ref.at[m, other, pl.ds(0, whole_rows)],
            dst_ref=main_v.at[m, other],
            send_sem=main_send.at[m, other],
            recv_sem=main_recv.at[m, other],
            device_id={"expert": other},
            device_id_type=MESH,
        )

    def own_main(m):
        return pltpu.make_async_copy(
            grads_ref.at[m, expert, pl.ds(0, whole_rows)], main_v.at[m, expert], main_own.at[m]
        )

    own_tail = pltpu.make_async_copy(tail_ref.at[expert], tail_v.at[expert], tail_own)

    if rest:
        for distance in range(1, n_expert):
            tail_copy(distance).start()
        own_tail.start()
    if whole_rows:
        for m in range(micro):
            for distance in range(1, n_expert):
                main_copy(m, distance).start()
            own_main(m).start()

    wpart_v[...] = jnp.zeros_like(wpart_v)
    for load in loads:
        load.wait()

    weight = weight_ref[...]
    earlier = (
        lax.broadcasted_iota(jnp.int32, (rows, rows), 0)
        > lax.broadcasted_iota(jnp.int32, (rows, rows), 1)
    ).astype(jnp.bfloat16)
    expert_ids = lax.broadcasted_iota(jnp.int32, (rows, experts), 1)

    def regroup(i, carry):
        m, cols = i // (width // tile), pl.ds(pl.multiple_of(lax.rem(i, width // tile) * tile, tile), tile)
        saved_v[m, :, cols] = pairs_v[m, :, :, cols].reshape(2 * rows, tile)
        return carry

    def route(m, carry):
        logits = lax.dot_general(
            normed_v[m], weight, (((1,), (1,)), ((), ())), preferred_element_type=jnp.float32
        )
        expl = jnp.exp(logits)
        probs = expl / jnp.sum(expl, axis=-1, keepdims=True)
        probs_v[m] = probs
        named = routes_ref[m]
        first = (named[:, 0:1] == expert_ids).astype(jnp.float32)
        second = (named[:, 1:2] == expert_ids).astype(jnp.float32)
        chosen_v[m, 0] = first
        chosen_v[m, 1] = second
        either = first + second
        before = jnp.dot(earlier, either.astype(jnp.bfloat16), preferred_element_type=jnp.float32)
        slot = jnp.where(either > 0.5, before.astype(jnp.int32), -1)
        parts = []
        if whole_rows:
            ids = lax.broadcasted_iota(jnp.int32, (rows, whole_rows), 1)
            for e in range(experts):
                parts.append(jnp.where(slot[:, e : e + 1] == ids, probs[:, e : e + 1], 0.0))
        if rest:
            ids = lax.broadcasted_iota(jnp.int32, (rows, tail_rows), 1)
            for e in range(experts):
                at = slot[:, e : e + 1]
                there = jnp.where(at >= whole_rows, at - whole_rows + m * rest, -1)
                parts.append(jnp.where(there == ids, probs[:, e : e + 1], 0.0))
        pick = jnp.concatenate(parts, axis=1)
        high = pick.astype(jnp.bfloat16)
        low = (pick - high.astype(jnp.float32)).astype(jnp.bfloat16)
        pick_v[m, pl.ds(0, rows)] = high
        pick_v[m, pl.ds(rows, rows)] = low
        return carry

    lax.fori_loop(0, micro, route, 0)
    lax.fori_loop(0, micro * (width // tile), regroup, 0)

    if rest:
        for distance in range(1, n_expert):
            tail_arrival(distance).wait_recv()
        own_tail.wait()

    @pl.when(pipe == n_pipe - 1)
    def _():
        top_load.wait()

    main_columns = experts * whole_rows
    pair = lax.broadcasted_iota(jnp.int32, (PACK, 2 * PACK), 1) - 2 * lax.broadcasted_iota(
        jnp.int32, (PACK, 2 * PACK), 0
    )

    def relay(m, q):
        part = pl.ds(pl.multiple_of(q * PACK, PACK), PACK)
        return pltpu.make_async_remote_copy(
            src_ref=out_ref.at[m, part],
            dst_ref=inc_v.at[m, part],
            send_sem=relay_send.at[m, q],
            recv_sem=relay_recv.at[m, q],
            device_id={"pipe": jnp.maximum(pipe - 1, 0)},
            device_id_type=MESH,
        )

    def block(m, carry):
        if whole_rows:
            for distance in range(1, n_expert):
                main_arrival(m, distance).wait_recv()
            own_main(m).wait()
        pick = pick_v[m]

        def combine(i, inner):
            cols = pl.ds(pl.multiple_of(i * tile, tile), tile)
            both = jnp.zeros((2 * rows, tile), jnp.float32)
            if whole_rows:
                both += jnp.dot(
                    pick[:, :main_columns],
                    main_v[m, :, :, cols].reshape(main_columns, tile),
                    preferred_element_type=jnp.float32,
                )
            if rest:
                both += jnp.dot(
                    pick[:, main_columns:],
                    tail_v[:, :, cols].reshape(experts * tail_rows, tile),
                    preferred_element_type=jnp.float32,
                )
            total_v[:, cols] = both[:rows] + both[rows:]
            return inner

        lax.fori_loop(0, width // tile, combine, 0)

        def step(q, inner):
            part = pl.ds(pl.multiple_of(q * PACK, PACK), PACK)

            @pl.when(pipe < n_pipe - 1)
            def _():
                relay(m, q).wait_recv()

            cross = lax.dot_general(
                inc_v[m, part],
                saved_v[m, pl.ds(pl.multiple_of(q * 2 * PACK, 2 * PACK), 2 * PACK)],
                (((1,), (1,)), ((), ())),
                preferred_element_type=jnp.float32,
            )
            probs = probs_v[m, part]
            weighted = jnp.zeros((PACK, experts), jnp.float32)
            for k in range(2):
                dot = jnp.sum(jnp.where(pair == k, cross, 0.0), axis=1, keepdims=True)
                weighted += dot * probs * chosen_v[m, k, part]
            dense = (weighted - probs * jnp.sum(weighted, axis=1, keepdims=True)).astype(jnp.bfloat16)
            dense_v[part] = dense

            def finish(i, innermost):
                cols = pl.ds(pl.multiple_of(i * tile, tile), tile)
                term = jnp.dot(dense, weight_ref[:, cols], preferred_element_type=jnp.float32)
                whole = inc_v[m, part, cols].astype(jnp.float32) + total_v[part, cols] + term
                out_ref[m, part, cols] = whole.astype(jnp.bfloat16)
                return innermost

            lax.fori_loop(0, width // tile, finish, 0, unroll=True)

            @pl.when(pipe > 0)
            def _():
                relay(m, q).start()

            return inner

        lax.fori_loop(0, rows // PACK, step, 0)
        dense = dense_v[...]

        def weigh(i, inner):
            cols = pl.ds(pl.multiple_of(i * chunk, chunk), chunk)
            wpart_v[i] += lax.dot_general(
                dense,
                normed_v[m, :, cols],
                (((0,), (0,)), ((), ())),
                preferred_element_type=jnp.float32,
            )
            return inner

        lax.fori_loop(0, chunks, weigh, 0)
        return carry

    lax.fori_loop(0, micro, block, 0)

    def part_copy(distance):
        other, place = member(distance)
        return pltpu.make_async_remote_copy(
            src_ref=wpart_v.at[jnp.minimum(other, chunks - 1)],
            dst_ref=wrecv_v.at[me],
            send_sem=part_send.at[other],
            recv_sem=part_recv.at[me],
            device_id=place,
            device_id_type=MESH,
        ), other

    def part_arrival(distance):
        other, place = member(distance)
        return pltpu.make_async_remote_copy(
            src_ref=wpart_v.at[0],
            dst_ref=wrecv_v.at[other],
            send_sem=part_send.at[other],
            recv_sem=part_recv.at[other],
            device_id=place,
            device_id_type=MESH,
        )

    def sum_copy(distance):
        other, place = member(distance)
        spot = jnp.minimum(me, chunks - 1)
        return pltpu.make_async_remote_copy(
            src_ref=wgrad_ref.at[spot],
            dst_ref=wgrad_ref.at[spot],
            send_sem=sum_send.at[other],
            recv_sem=sum_recv.at[me],
            device_id=place,
            device_id_type=MESH,
        )

    def sum_arrival(distance):
        other, place = member(distance)
        spot = jnp.minimum(other, chunks - 1)
        return pltpu.make_async_remote_copy(
            src_ref=wgrad_ref.at[spot],
            dst_ref=wgrad_ref.at[spot],
            send_sem=sum_send.at[other],
            recv_sem=sum_recv.at[other],
            device_id=place,
            device_id_type=MESH,
        ), other

    for distance in range(1, group):
        copy, other = part_copy(distance)

        @pl.when(other < chunks)
        def _():
            copy.start()

    @pl.when(me < chunks)
    def _():
        total = wpart_v[me]
        for distance in range(1, group):
            part_arrival(distance).wait_recv()
            total += wrecv_v[member(distance)[0]]
        wgrad_ref[me] = total * (1.0 / micro)
        for distance in range(1, group):
            sum_copy(distance).start()

    for distance in range(1, group):
        copy, other = sum_arrival(distance)

        @pl.when(other < chunks)
        def _():
            copy.wait_recv()

    if rest:
        for distance in range(1, n_expert):
            tail_copy(distance).wait_send()
    if whole_rows:
        for m in range(micro):
            for distance in range(1, n_expert):
                main_copy(m, distance).wait_send()

    @pl.when(pipe > 0)
    def _():
        for m in range(micro):
            for q in range(rows // PACK):
                relay(m, q).wait_send()

    for distance in range(1, group):
        copy, other = part_copy(distance)

        @pl.when(other < chunks)
        def _():
            copy.wait_send()

    @pl.when(me < chunks)
    def _():
        for distance in range(1, group):
            sum_copy(distance).wait_send()


def on_device(sizes, normed, saved_out, expert_grads, routes, router_weight, upstream):
    n_pipe, n_expert, n_dp = sizes
    micro, rows, width = normed.shape[1:]
    experts = router_weight.shape[2]
    capacity = expert_grads.shape[5]
    whole_rows = capacity // PACK * PACK
    rest = capacity - whole_rows
    tail_rows = -(-max(rest * micro, 1) // PACK) * PACK
    group = n_expert * n_dp
    chunks = min(group, width // 128)
    chunk = width // chunks
    grads = expert_grads.reshape(micro, n_expert, capacity, width)
    tail = jnp.transpose(grads[:, :, whole_rows:], (1, 0, 2, 3)).reshape(n_expert, rest * micro, width)
    tail = jnp.pad(tail, ((0, 0), (0, tail_rows - rest * micro), (0, 0)))
    columns = experts * (whole_rows + (tail_rows if rest else 0))
    any_space = pl.BlockSpec(memory_space=pl.ANY)
    vmem = pl.BlockSpec(memory_space=pltpu.VMEM)
    dma = pltpu.SemaphoreType.DMA
    out, wgrad = pl.pallas_call(
        functools.partial(kernel, sizes),
        out_shape=(
            jax.ShapeDtypeStruct((micro, rows, width), jnp.bfloat16),
            jax.ShapeDtypeStruct((chunks, experts, chunk), jnp.float32),
        ),
        in_specs=[any_space] * 5 + [vmem] * 2,
        out_specs=(vmem, vmem),
        scratch_shapes=[
            pltpu.VMEM((micro, n_expert, max(whole_rows, PACK), width), jnp.bfloat16),
            pltpu.VMEM((n_expert, tail_rows, width), jnp.bfloat16),
            pltpu.VMEM((micro, rows, width), jnp.bfloat16),
            pltpu.VMEM((micro, rows, 2, width), jnp.bfloat16),
            pltpu.VMEM((micro, 2 * rows, width), jnp.bfloat16),
            pltpu.VMEM((micro, rows, width), jnp.bfloat16),
            pltpu.VMEM((rows, width), jnp.float32),
            pltpu.VMEM((rows, experts), jnp.bfloat16),
            pltpu.VMEM((micro, 2 * rows, columns), jnp.bfloat16),
            pltpu.VMEM((micro, rows, experts), jnp.float32),
            pltpu.VMEM((micro, 2, rows, experts), jnp.float32),
            pltpu.VMEM((chunks, experts, chunk), jnp.float32),
            pltpu.VMEM((group, experts, chunk), jnp.float32),
            dma((micro, n_expert)),
            dma((micro, n_expert)),
            dma((n_expert,)),
            dma((n_expert,)),
            dma((micro,)),
            dma,
            dma((2,)),
            dma,
            dma((micro, rows // PACK)),
            dma((micro, rows // PACK)),
            dma((group,)),
            dma((group,)),
            dma((group,)),
            dma((group,)),
        ],
        compiler_params=pltpu.CompilerParams(
            collective_id=0, has_side_effects=True, vmem_limit_bytes=28 * 2**20
        ),
        name="relay",
    )(
        grads,
        tail,
        normed[0],
        saved_out[0],
        upstream,
        routes[0],
        router_weight[0].T,
    )
    router_grad = jnp.transpose(wgrad, (0, 2, 1)).reshape(width, experts)
    return (out[None], router_grad[None])


def solution(mesh):
    in_specs = (
        P("pipe", None, ("expert", "dp"), None),
        P("pipe", None, ("expert", "dp"), None, None),
        P("pipe", None, "dp", "expert", None, None, None),
        P("pipe", None, ("expert", "dp"), None),
        P("pipe", None, None),
        P(None, ("expert", "dp"), None),
    )
    out_specs = (P("pipe", None, ("expert", "dp"), None), P("pipe", None, None))
    sizes = (mesh.shape["pipe"], mesh.shape["expert"], mesh.shape["dp"])
    return jax.shard_map(
        functools.partial(on_device, sizes),
        mesh=mesh,
        in_specs=in_specs,
        out_specs=out_specs,
        check_vma=False,
    )
```

```python
import functools

import jax
import jax.numpy as jnp
from jax import lax
from jax.experimental import pallas as pl
from jax.experimental.pallas import tpu as pltpu
from jax.sharding import PartitionSpec as P

MESH = pl.DeviceIdType.MESH
PACK = 16


def kernel(
    sizes,
    grads_ref,
    normed_ref,
    saved_ref,
    upstream_ref,
    routes_ref,
    weight_ref,
    out_ref,
    wgrad_ref,
    grads_v,
    main_v,
    tail_v,
    mate_main_v,
    mate_tail_v,
    sums_v,
    terms_v,
    normed_v,
    pairs_v,
    saved_v,
    inc_v,
    total_v,
    dense_v,
    pick_v,
    asked_v,
    probs_v,
    chosen_v,
    wpart_v,
    wrecv_v,
    grads_sem,
    main_send,
    main_recv,
    tail_send,
    tail_recv,
    pick_send,
    pick_recv,
    term_send,
    term_recv,
    load_sem,
    top_sem,
    relay_send,
    relay_recv,
    part_send,
    part_recv,
    sum_send,
    sum_recv,
):
    n_pipe, n_expert, n_dp = sizes
    micro, rows, width = normed_v.shape
    experts = weight_ref.shape[0]
    capacity = grads_ref.shape[1]
    whole_rows = capacity // PACK * PACK
    rest = capacity - whole_rows
    tail_rows = tail_v.shape[1]
    columns = pick_v.shape[3]
    n_pairs = n_expert // 2
    group = n_expert * n_dp
    chunks, _, chunk = wpart_v.shape
    tile = min(width, 512)
    pipe = lax.axis_index("pipe")
    expert = lax.axis_index("expert")
    dp = lax.axis_index("dp")
    me = expert * n_dp + dp
    pair = expert // 2
    odd = lax.rem(expert, 2)
    mate = expert + 1 - 2 * odd

    def summed_here(j):
        return ((odd == 1) & (j > expert)) | ((odd == 0) & (j < expert))

    def member(distance):
        other = lax.rem(me + distance, group)
        return other, {"expert": other // n_dp, "dp": lax.rem(other, n_dp)}

    barrier = pltpu.get_barrier_semaphore()
    for distance in range(1, group):
        _, place = member(distance)
        pl.semaphore_signal(barrier, inc=1, device_id=place, device_id_type=MESH)

    @pl.when(pipe > 0)
    def _():
        pl.semaphore_signal(barrier, inc=1, device_id={"pipe": pipe - 1}, device_id_type=MESH)

    @pl.when(pipe < n_pipe - 1)
    def _():
        pl.semaphore_signal(barrier, inc=1, device_id={"pipe": pipe + 1}, device_id_type=MESH)

    def grads_load(m):
        return pltpu.make_async_copy(grads_ref.at[m], grads_v.at[m], grads_sem.at[m])

    for m in range(micro):
        grads_load(m).start()
    loads = [
        pltpu.make_async_copy(normed_ref, normed_v, load_sem.at[0]),
        pltpu.make_async_copy(saved_ref, pairs_v, load_sem.at[1]),
    ]
    top_load = pltpu.make_async_copy(upstream_ref, inc_v, top_sem)
    for load in loads:
        load.start()

    @pl.when(pipe == n_pipe - 1)
    def _():
        top_load.start()

    pl.semaphore_wait(
        barrier,
        group - 1 + jnp.where(pipe > 0, 1, 0) + jnp.where(pipe < n_pipe - 1, 1, 0),
    )

    def tail_copy(j):
        return pltpu.make_async_remote_copy(
            src_ref=tail_v.at[j],
            dst_ref=mate_tail_v.at[j],
            send_sem=tail_send.at[j],
            recv_sem=tail_recv.at[j],
            device_id={"expert": mate},
            device_id_type=MESH,
        )

    def main_copy(m, j):
        return pltpu.make_async_remote_copy(
            src_ref=main_v.at[m, j],
            dst_ref=mate_main_v.at[m, j],
            send_sem=main_send.at[m, j],
            recv_sem=main_recv.at[m, j],
            device_id={"expert": mate},
            device_id_type=MESH,
        )

    def first_of(p):
        return jnp.where(p == pair, expert, jnp.where(p < pair, 2 * p + 1, 2 * p))

    def pick_copy(p):
        return pltpu.make_async_remote_copy(
            src_ref=pick_v.at[p],
            dst_ref=asked_v.at[expert],
            send_sem=pick_send.at[p],
            recv_sem=pick_recv.at[expert],
            device_id={"expert": first_of(p)},
            device_id_type=MESH,
        )

    def pick_arrival(j):
        return pltpu.make_async_remote_copy(
            src_ref=pick_v.at[0],
            dst_ref=asked_v.at[j],
            send_sem=pick_send.at[0],
            recv_sem=pick_recv.at[j],
            device_id={"expert": j},
            device_id_type=MESH,
        )

    def term_copy(m, j):
        return pltpu.make_async_remote_copy(
            src_ref=sums_v.at[lax.rem(m, 2), j],
            dst_ref=terms_v.at[m, pair],
            send_sem=term_send.at[m, j],
            recv_sem=term_recv.at[m, pair],
            device_id={"expert": j},
            device_id_type=MESH,
        )

    def term_arrival(m, p):
        return pltpu.make_async_remote_copy(
            src_ref=sums_v.at[0, 0],
            dst_ref=terms_v.at[m, p],
            send_sem=term_send.at[m, 0],
            recv_sem=term_recv.at[m, p],
            device_id={"expert": first_of(p)},
            device_id_type=MESH,
        )

    def far(t):
        j = jnp.where(odd == 1, t, n_expert - 1 - t)
        return j, (j != expert) & (j != mate) & jnp.logical_not(summed_here(j))

    tiles = width // tile

    def columns_of(i):
        return pl.ds(pl.multiple_of(i * tile, tile), tile)

    if rest:
        shape = (n_expert * tail_rows, micro * rest * n_expert)
        row, col = (lax.broadcasted_iota(jnp.int32, shape, axis) for axis in (0, 1))
        tail_order = (
            col == lax.rem(row, tail_rows) * n_expert + lax.div(row, tail_rows)
        ).astype(jnp.bfloat16)
    if whole_rows:
        shape = (n_expert * whole_rows, n_expert * whole_rows)
        row, col = (lax.broadcasted_iota(jnp.int32, shape, axis) for axis in (0, 1))
        main_order = (
            col == lax.rem(row, whole_rows) * n_expert + lax.div(row, whole_rows)
        ).astype(jnp.bfloat16)

    def regroup_tail(i, carry):
        cols = columns_of(i)
        slots = jnp.concatenate(
            [
                grads_v[m, whole_rows:, :, cols].reshape(rest * n_expert, tile)
                for m in range(micro)
            ],
            axis=0,
        )
        ordered = jnp.dot(tail_order, slots, preferred_element_type=jnp.float32)
        tail_v[:, :, cols] = ordered.astype(jnp.bfloat16).reshape(n_expert, tail_rows, tile)
        return carry

    def regroup_main(m):
        def regroup(i, carry):
            cols = columns_of(i)
            slots = grads_v[m, :whole_rows, :, cols].reshape(whole_rows * n_expert, tile)
            ordered = jnp.dot(main_order, slots, preferred_element_type=jnp.float32)
            main_v[m, :, :, cols] = ordered.astype(jnp.bfloat16).reshape(
                n_expert, whole_rows, tile
            )
            return carry

        lax.fori_loop(0, tiles, regroup, 0)

    for m in range(micro):
        grads_load(m).wait()
    if rest:
        lax.fori_loop(0, tiles, regroup_tail, 0)
    if whole_rows:
        regroup_main(0)
    for t in range(n_expert):
        j, send = far(t)

        @pl.when(send)
        def _():
            if rest:
                tail_copy(j).start()
            if whole_rows:
                main_copy(0, j).start()

    wpart_v[...] = jnp.zeros_like(wpart_v)
    for load in loads:
        load.wait()

    weight = weight_ref[...]
    earlier = (
        lax.broadcasted_iota(jnp.int32, (rows, rows), 0)
        > lax.broadcasted_iota(jnp.int32, (rows, rows), 1)
    ).astype(jnp.bfloat16)
    expert_ids = lax.broadcasted_iota(jnp.int32, (rows, experts), 1)

    def regroup(i, carry):
        m, cols = i // (width // tile), pl.ds(pl.multiple_of(lax.rem(i, width // tile) * tile, tile), tile)
        saved_v[m, :, cols] = pairs_v[m, :, :, cols].reshape(2 * rows, tile)
        return carry

    def route(m, carry):
        logits = lax.dot_general(
            normed_v[m], weight, (((1,), (1,)), ((), ())), preferred_element_type=jnp.float32
        )
        expl = jnp.exp(logits)
        probs = expl / jnp.sum(expl, axis=-1, keepdims=True)
        probs_v[m] = probs
        named = routes_ref[m]
        first = (named[:, 0:1] == expert_ids).astype(jnp.float32)
        second = (named[:, 1:2] == expert_ids).astype(jnp.float32)
        chosen_v[m, 0] = first
        chosen_v[m, 1] = second
        either = first + second
        before = jnp.dot(earlier, either.astype(jnp.bfloat16), preferred_element_type=jnp.float32)
        slot = jnp.where(either > 0.5, before.astype(jnp.int32), -1)
        ids = lax.broadcasted_iota(jnp.int32, (rows, columns), 1)
        for p in range(n_pairs):
            first_expert = first_of(p)
            pick = jnp.zeros((rows, columns), jnp.float32)
            for place, e in enumerate((first_expert, 4 * p + 1 - first_expert)):
                this = expert_ids == e
                at = jnp.sum(jnp.where(this, slot, 0), axis=1, keepdims=True)
                gate = jnp.sum(jnp.where(this, probs, 0.0), axis=1, keepdims=True)
                late = 2 * whole_rows + place * tail_rows + at - whole_rows + m * rest
                there = jnp.where(at < whole_rows, at + place * whole_rows, late)
                there = jnp.where(at < 0, -1, there)
                pick += jnp.where(there == ids, gate, 0.0)
            high = pick.astype(jnp.bfloat16)
            low = (pick - high.astype(jnp.float32)).astype(jnp.bfloat16)
            pick_v[p, m, pl.ds(0, rows)] = high
            pick_v[p, m, pl.ds(rows, rows)] = low
        return carry

    lax.fori_loop(0, micro, route, 0)
    for p in range(n_pairs):

        @pl.when(p != pair)
        def _():
            pick_copy(p).start()

    def send_near(m):
        if rest and m == 0:
            tail_copy(mate).start()
        if whole_rows:
            main_copy(m, mate).start()

    for m in range(1, micro):
        if whole_rows:
            regroup_main(m)
            for t in range(n_expert):
                j, send = far(t)

                @pl.when(send)
                def _():
                    main_copy(m, j).start()

        send_near(m - 1)
    send_near(micro - 1)

    lax.fori_loop(0, micro * (width // tile), regroup, 0)

    @pl.when(pipe == n_pipe - 1)
    def _():
        top_load.wait()

    def await_slots(m, j):
        if whole_rows:
            main_copy(m, j).wait_recv()
        if rest:

            @pl.when(m == 0)
            def _():
                tail_copy(j).wait_recv()

    def picked(m, j, pick, cols):
        slots = []
        if whole_rows:
            slots += [main_v[m, j, :, cols], mate_main_v[m, j, :, cols]]
        if rest:
            slots += [tail_v[j, :, cols], mate_tail_v[j, :, cols]]
        both = jnp.dot(
            pick, jnp.concatenate(slots, axis=0), preferred_element_type=jnp.float32
        )
        return both[:rows] + both[rows:]

    def sum_for_others(m):
        def one(t, carry):
            j = jnp.where(odd == 1, n_expert - 1 - t, t)

            @pl.when(summed_here(j))
            def _():
                await_slots(m, j)

                @pl.when(m == 0)
                def _():
                    pick_arrival(j).wait_recv()

                @pl.when(m >= 2)
                def _():
                    term_copy(m - 2, j).wait_send()

                pick = asked_v[j, m]

                def combine(i, inner):
                    cols = columns_of(i)
                    sums_v[lax.rem(m, 2), j, :, cols] = picked(m, j, pick, cols).astype(
                        jnp.bfloat16
                    )
                    return inner

                lax.fori_loop(0, tiles, combine, 0)
                term_copy(m, j).start()

            return carry

        lax.fori_loop(0, n_expert, one, 0)

    offset = lax.broadcasted_iota(jnp.int32, (PACK, 2 * PACK), 1) - 2 * lax.broadcasted_iota(
        jnp.int32, (PACK, 2 * PACK), 0
    )

    def relay(m, q):
        part = pl.ds(pl.multiple_of(q * PACK, PACK), PACK)
        return pltpu.make_async_remote_copy(
            src_ref=out_ref.at[m, part],
            dst_ref=inc_v.at[m, part],
            send_sem=relay_send.at[m, q],
            recv_sem=relay_recv.at[m, q],
            device_id={"pipe": jnp.maximum(pipe - 1, 0)},
            device_id_type=MESH,
        )

    def block(m):
        await_slots(m, expert)
        pick = pick_v[pair, m]

        def combine(i, inner):
            cols = columns_of(i)
            total_v[:, cols] = picked(m, expert, pick, cols)
            return inner

        lax.fori_loop(0, tiles, combine, 0)

        def join(p, carry):
            @pl.when(p != pair)
            def _():
                term_arrival(m, p).wait_recv()

                def add(i, inner):
                    cols = columns_of(i)
                    total_v[:, cols] += terms_v[m, p, :, cols].astype(jnp.float32)
                    return inner

                lax.fori_loop(0, tiles, add, 0)

            return carry

        lax.fori_loop(0, n_pairs, join, 0)

        def step(q, inner):
            part = pl.ds(pl.multiple_of(q * PACK, PACK), PACK)

            @pl.when(pipe < n_pipe - 1)
            def _():
                relay(m, q).wait_recv()

            cross = lax.dot_general(
                inc_v[m, part],
                saved_v[m, pl.ds(pl.multiple_of(q * 2 * PACK, 2 * PACK), 2 * PACK)],
                (((1,), (1,)), ((), ())),
                preferred_element_type=jnp.float32,
            )
            probs = probs_v[m, part]
            weighted = jnp.zeros((PACK, experts), jnp.float32)
            for k in range(2):
                dot = jnp.sum(jnp.where(offset == k, cross, 0.0), axis=1, keepdims=True)
                weighted += dot * probs * chosen_v[m, k, part]
            dense = (weighted - probs * jnp.sum(weighted, axis=1, keepdims=True)).astype(jnp.bfloat16)
            dense_v[part] = dense

            def finish(i, innermost):
                cols = pl.ds(pl.multiple_of(i * tile, tile), tile)
                term = jnp.dot(dense, weight_ref[:, cols], preferred_element_type=jnp.float32)
                whole = inc_v[m, part, cols].astype(jnp.float32) + total_v[part, cols] + term
                out_ref[m, part, cols] = whole.astype(jnp.bfloat16)
                return innermost

            lax.fori_loop(0, width // tile, finish, 0, unroll=True)

            @pl.when(pipe > 0)
            def _():
                relay(m, q).start()

            return inner

        lax.fori_loop(0, rows // PACK, step, 0)
        dense = dense_v[...]

        def weigh(i, inner):
            cols = pl.ds(pl.multiple_of(i * chunk, chunk), chunk)
            wpart_v[i] += lax.dot_general(
                dense,
                normed_v[m, :, cols],
                (((0,), (0,)), ((), ())),
                preferred_element_type=jnp.float32,
            )
            return inner

        lax.fori_loop(0, chunks, weigh, 0)

    def turn(m, carry):
        @pl.when(m < micro)
        def _():
            sum_for_others(m)

        @pl.when(m > 0)
        def _():
            block(m - 1)

        return carry

    lax.fori_loop(0, micro + 1, turn, 0)

    def part_copy(distance):
        other, place = member(distance)
        return pltpu.make_async_remote_copy(
            src_ref=wpart_v.at[jnp.minimum(other, chunks - 1)],
            dst_ref=wrecv_v.at[me],
            send_sem=part_send.at[other],
            recv_sem=part_recv.at[me],
            device_id=place,
            device_id_type=MESH,
        ), other

    def part_arrival(distance):
        other, place = member(distance)
        return pltpu.make_async_remote_copy(
            src_ref=wpart_v.at[0],
            dst_ref=wrecv_v.at[other],
            send_sem=part_send.at[other],
            recv_sem=part_recv.at[other],
            device_id=place,
            device_id_type=MESH,
        )

    def sum_copy(distance):
        other, place = member(distance)
        spot = jnp.minimum(me, chunks - 1)
        return pltpu.make_async_remote_copy(
            src_ref=wgrad_ref.at[spot],
            dst_ref=wgrad_ref.at[spot],
            send_sem=sum_send.at[other],
            recv_sem=sum_recv.at[me],
            device_id=place,
            device_id_type=MESH,
        )

    def sum_arrival(distance):
        other, place = member(distance)
        spot = jnp.minimum(other, chunks - 1)
        return pltpu.make_async_remote_copy(
            src_ref=wgrad_ref.at[spot],
            dst_ref=wgrad_ref.at[spot],
            send_sem=sum_send.at[other],
            recv_sem=sum_recv.at[other],
            device_id=place,
            device_id_type=MESH,
        ), other

    for distance in range(1, group):
        copy, other = part_copy(distance)

        @pl.when(other < chunks)
        def _():
            copy.start()

    @pl.when(me < chunks)
    def _():
        total = wpart_v[me]
        for distance in range(1, group):
            part_arrival(distance).wait_recv()
            total += wrecv_v[member(distance)[0]]
        wgrad_ref[me] = total * (1.0 / micro)
        for distance in range(1, group):
            sum_copy(distance).start()

    for distance in range(1, group):
        copy, other = sum_arrival(distance)

        @pl.when(other < chunks)
        def _():
            copy.wait_recv()

    for j in range(n_expert):

        @pl.when((expert != j) & jnp.logical_not(summed_here(j)))
        def _():
            if rest:
                tail_copy(j).wait_send()
            if whole_rows:
                for m in range(micro):
                    main_copy(m, j).wait_send()

        @pl.when(summed_here(j))
        def _():
            for m in range(max(micro - 2, 0), micro):
                term_copy(m, j).wait_send()

    for p in range(n_pairs):

        @pl.when(p != pair)
        def _():
            pick_copy(p).wait_send()

    @pl.when(pipe > 0)
    def _():
        for m in range(micro):
            for q in range(rows // PACK):
                relay(m, q).wait_send()

    for distance in range(1, group):
        copy, other = part_copy(distance)

        @pl.when(other < chunks)
        def _():
            copy.wait_send()

    @pl.when(me < chunks)
    def _():
        for distance in range(1, group):
            sum_copy(distance).wait_send()


def on_device(sizes, normed, saved_out, expert_grads, routes, router_weight, upstream):
    n_pipe, n_expert, n_dp = sizes
    micro, rows, width = normed.shape[1:]
    experts = router_weight.shape[2]
    capacity = expert_grads.shape[5]
    whole_rows = capacity // PACK * PACK
    rest = capacity - whole_rows
    tail_rows = -(-max(rest * micro, 1) // PACK) * PACK
    group = n_expert * n_dp
    chunks = min(group, width // 128)
    chunk = width // chunks
    grads = jnp.swapaxes(expert_grads.reshape(micro, n_expert, capacity, width), 1, 2)
    columns = 2 * (whole_rows + (tail_rows if rest else 0))
    main_shape = (
        (micro, n_expert, whole_rows, width) if whole_rows else (1, 1, PACK, width)
    )
    tail_shape = (n_expert, tail_rows, width) if rest else (1, tail_rows, width)
    n_pairs = n_expert // 2
    any_space = pl.BlockSpec(memory_space=pl.ANY)
    vmem = pl.BlockSpec(memory_space=pltpu.VMEM)
    dma = pltpu.SemaphoreType.DMA
    out, wgrad = pl.pallas_call(
        functools.partial(kernel, sizes),
        out_shape=(
            jax.ShapeDtypeStruct((micro, rows, width), jnp.bfloat16),
            jax.ShapeDtypeStruct((chunks, experts, chunk), jnp.float32),
        ),
        in_specs=[any_space] * 4 + [vmem] * 2,
        out_specs=(vmem, vmem),
        scratch_shapes=[
            pltpu.VMEM((micro, capacity, n_expert, width), jnp.bfloat16),
            pltpu.VMEM(main_shape, jnp.bfloat16),
            pltpu.VMEM(tail_shape, jnp.bfloat16),
            pltpu.VMEM(main_shape, jnp.bfloat16),
            pltpu.VMEM(tail_shape, jnp.bfloat16),
            pltpu.VMEM((2, n_expert, rows, width), jnp.bfloat16),
            pltpu.VMEM((micro, n_pairs, rows, width), jnp.bfloat16),
            pltpu.VMEM((micro, rows, width), jnp.bfloat16),
            pltpu.VMEM((micro, rows, 2, width), jnp.bfloat16),
            pltpu.VMEM((micro, 2 * rows, width), jnp.bfloat16),
            pltpu.VMEM((micro, rows, width), jnp.bfloat16),
            pltpu.VMEM((rows, width), jnp.float32),
            pltpu.VMEM((rows, experts), jnp.bfloat16),
            pltpu.VMEM((n_pairs, micro, 2 * rows, columns), jnp.bfloat16),
            pltpu.VMEM((n_expert, micro, 2 * rows, columns), jnp.bfloat16),
            pltpu.VMEM((micro, rows, experts), jnp.float32),
            pltpu.VMEM((micro, 2, rows, experts), jnp.float32),
            pltpu.VMEM((chunks, experts, chunk), jnp.float32),
            pltpu.VMEM((group, experts, chunk), jnp.float32),
            dma((micro,)),
            dma((micro, n_expert)),
            dma((micro, n_expert)),
            dma((n_expert,)),
            dma((n_expert,)),
            dma((n_pairs,)),
            dma((n_expert,)),
            dma((micro, n_expert)),
            dma((micro, n_pairs)),
            dma((2,)),
            dma,
            dma((micro, rows // PACK)),
            dma((micro, rows // PACK)),
            dma((group,)),
            dma((group,)),
            dma((group,)),
            dma((group,)),
        ],
        compiler_params=pltpu.CompilerParams(
            collective_id=0, has_side_effects=True, vmem_limit_bytes=60 * 2**20
        ),
        name="relay",
    )(
        grads,
        normed[0],
        saved_out[0],
        upstream,
        routes[0],
        router_weight[0].T,
    )
    router_grad = jnp.transpose(wgrad, (0, 2, 1)).reshape(width, experts)
    return (out[None], router_grad[None])


def solution(mesh):
    in_specs = (
        P("pipe", None, ("expert", "dp"), None),
        P("pipe", None, ("expert", "dp"), None, None),
        P("pipe", None, "dp", "expert", None, None, None),
        P("pipe", None, ("expert", "dp"), None),
        P("pipe", None, None),
        P(None, ("expert", "dp"), None),
    )
    out_specs = (P("pipe", None, ("expert", "dp"), None), P("pipe", None, None))
    sizes = (mesh.shape["pipe"], mesh.shape["expert"], mesh.shape["dp"])
    return jax.shard_map(
        functools.partial(on_device, sizes),
        mesh=mesh,
        in_specs=in_specs,
        out_specs=out_specs,
        check_vma=False,
    )
```

```python
import functools

import jax
import jax.numpy as jnp
from jax import lax
from jax.experimental import pallas as pl
from jax.experimental.pallas import tpu as pltpu
from jax.sharding import PartitionSpec as P

MESH = pl.DeviceIdType.MESH
PACK = 16


def kernel(
    sizes,
    grads_ref,
    normed_ref,
    saved_ref,
    upstream_ref,
    routes_ref,
    weight_ref,
    out_ref,
    wgrad_ref,
    grads_v,
    main_v,
    tail_v,
    mate_main_v,
    mate_tail_v,
    sums_v,
    terms_v,
    normed_v,
    pairs_v,
    saved_v,
    inc_v,
    total_v,
    dense_v,
    pick_v,
    asked_v,
    probs_v,
    chosen_v,
    wpart_v,
    wrecv_v,
    grads_sem,
    main_send,
    main_recv,
    tail_send,
    tail_recv,
    pick_send,
    pick_recv,
    term_send,
    term_recv,
    load_sem,
    top_sem,
    relay_send,
    relay_recv,
    part_send,
    part_recv,
    sum_send,
    sum_recv,
):
    n_pipe, n_expert, n_dp = sizes
    micro, rows, width = normed_v.shape
    experts = weight_ref.shape[0]
    capacity = grads_ref.shape[1]
    whole_rows = capacity // PACK * PACK
    rest = capacity - whole_rows
    tail_rows = tail_v.shape[1]
    columns = pick_v.shape[3]
    n_pairs = n_expert // 2
    group = n_expert * n_dp
    chunks, _, chunk = wpart_v.shape
    tile = min(width, 512)
    pipe = lax.axis_index("pipe")
    expert = lax.axis_index("expert")
    dp = lax.axis_index("dp")
    me = expert * n_dp + dp
    pair = expert // 2
    odd = lax.rem(expert, 2)
    mate = expert + 1 - 2 * odd

    def summed_here(j):
        return ((odd == 1) & (j > expert)) | ((odd == 0) & (j < expert))

    def member(distance):
        other = lax.rem(me + distance, group)
        return other, {"expert": other // n_dp, "dp": lax.rem(other, n_dp)}

    barrier = pltpu.get_barrier_semaphore()
    for distance in range(1, group):
        _, place = member(distance)
        pl.semaphore_signal(barrier, inc=1, device_id=place, device_id_type=MESH)

    @pl.when(pipe > 0)
    def _():
        pl.semaphore_signal(barrier, inc=1, device_id={"pipe": pipe - 1}, device_id_type=MESH)

    @pl.when(pipe < n_pipe - 1)
    def _():
        pl.semaphore_signal(barrier, inc=1, device_id={"pipe": pipe + 1}, device_id_type=MESH)

    def grads_load(m):
        return pltpu.make_async_copy(grads_ref.at[m], grads_v.at[m], grads_sem.at[m])

    for m in range(micro):
        grads_load(m).start()
    loads = [
        pltpu.make_async_copy(normed_ref, normed_v, load_sem.at[0]),
        pltpu.make_async_copy(saved_ref, pairs_v, load_sem.at[1]),
    ]
    top_load = pltpu.make_async_copy(upstream_ref, inc_v, top_sem)
    for load in loads:
        load.start()

    @pl.when(pipe == n_pipe - 1)
    def _():
        top_load.start()

    pl.semaphore_wait(
        barrier,
        group - 1 + jnp.where(pipe > 0, 1, 0) + jnp.where(pipe < n_pipe - 1, 1, 0),
    )

    def tail_copy(j):
        return pltpu.make_async_remote_copy(
            src_ref=tail_v.at[j],
            dst_ref=mate_tail_v.at[j],
            send_sem=tail_send.at[j],
            recv_sem=tail_recv.at[j],
            device_id={"expert": mate},
            device_id_type=MESH,
        )

    def main_copy(m, j):
        return pltpu.make_async_remote_copy(
            src_ref=main_v.at[m, j],
            dst_ref=mate_main_v.at[m, j],
            send_sem=main_send.at[m, j],
            recv_sem=main_recv.at[m, j],
            device_id={"expert": mate},
            device_id_type=MESH,
        )

    def first_of(p):
        return jnp.where(p == pair, expert, jnp.where(p < pair, 2 * p + 1, 2 * p))

    def pick_copy(p):
        return pltpu.make_async_remote_copy(
            src_ref=pick_v.at[p, :, pl.ds(0, rows)],
            dst_ref=asked_v.at[expert],
            send_sem=pick_send.at[p],
            recv_sem=pick_recv.at[expert],
            device_id={"expert": first_of(p)},
            device_id_type=MESH,
        )

    def pick_arrival(j):
        return pltpu.make_async_remote_copy(
            src_ref=pick_v.at[0, :, pl.ds(0, rows)],
            dst_ref=asked_v.at[j],
            send_sem=pick_send.at[0],
            recv_sem=pick_recv.at[j],
            device_id={"expert": j},
            device_id_type=MESH,
        )

    def term_copy(m, j):
        return pltpu.make_async_remote_copy(
            src_ref=sums_v.at[lax.rem(m, 2), j],
            dst_ref=terms_v.at[m, pair],
            send_sem=term_send.at[m, j],
            recv_sem=term_recv.at[m, pair],
            device_id={"expert": j},
            device_id_type=MESH,
        )

    def term_arrival(m, p):
        return pltpu.make_async_remote_copy(
            src_ref=sums_v.at[0, 0],
            dst_ref=terms_v.at[m, p],
            send_sem=term_send.at[m, 0],
            recv_sem=term_recv.at[m, p],
            device_id={"expert": first_of(p)},
            device_id_type=MESH,
        )

    def far(t):
        j = jnp.where(odd == 1, t, n_expert - 1 - t)
        return j, (j != expert) & (j != mate) & jnp.logical_not(summed_here(j))

    tiles = width // tile

    def columns_of(i):
        return pl.ds(pl.multiple_of(i * tile, tile), tile)

    if rest:
        shape = (n_expert * tail_rows, micro * rest * n_expert)
        row, col = (lax.broadcasted_iota(jnp.int32, shape, axis) for axis in (0, 1))
        tail_order = (
            col == lax.rem(row, tail_rows) * n_expert + lax.div(row, tail_rows)
        ).astype(jnp.bfloat16)
    if whole_rows:
        shape = (n_expert * whole_rows, n_expert * whole_rows)
        row, col = (lax.broadcasted_iota(jnp.int32, shape, axis) for axis in (0, 1))
        main_order = (
            col == lax.rem(row, whole_rows) * n_expert + lax.div(row, whole_rows)
        ).astype(jnp.bfloat16)

    def regroup_tail(i, carry):
        cols = columns_of(i)
        slots = jnp.concatenate(
            [
                grads_v[m, whole_rows:, :, cols].reshape(rest * n_expert, tile)
                for m in range(micro)
            ],
            axis=0,
        )
        ordered = jnp.dot(tail_order, slots, preferred_element_type=jnp.float32)
        tail_v[:, :, cols] = ordered.astype(jnp.bfloat16).reshape(n_expert, tail_rows, tile)
        return carry

    def regroup_main(m):
        def regroup(i, carry):
            cols = columns_of(i)
            slots = grads_v[m, :whole_rows, :, cols].reshape(whole_rows * n_expert, tile)
            ordered = jnp.dot(main_order, slots, preferred_element_type=jnp.float32)
            main_v[m, :, :, cols] = ordered.astype(jnp.bfloat16).reshape(
                n_expert, whole_rows, tile
            )
            return carry

        lax.fori_loop(0, tiles, regroup, 0, unroll=4)

    def send_first(t):
        j, send = far(t)

        @pl.when(send)
        def _():
            if rest:
                tail_copy(j).start()
            if whole_rows:
                main_copy(0, j).start()

    for m in range(micro):
        grads_load(m).wait()
    if rest:
        lax.fori_loop(0, tiles, regroup_tail, 0, unroll=4)
    if whole_rows:
        regroup_main(0)
    send_first(0)

    wpart_v[...] = jnp.zeros_like(wpart_v)
    for load in loads:
        load.wait()

    weight = weight_ref[...]
    earlier = (
        lax.broadcasted_iota(jnp.int32, (rows, rows), 0)
        > lax.broadcasted_iota(jnp.int32, (rows, rows), 1)
    ).astype(jnp.bfloat16)
    expert_ids = lax.broadcasted_iota(jnp.int32, (rows, experts), 1)

    def regroup(i, carry):
        m, cols = i // (width // tile), pl.ds(pl.multiple_of(lax.rem(i, width // tile) * tile, tile), tile)
        saved_v[m, :, cols] = pairs_v[m, :, :, cols].reshape(2 * rows, tile)
        return carry

    def route(m, carry):
        logits = lax.dot_general(
            normed_v[m], weight, (((1,), (1,)), ((), ())), preferred_element_type=jnp.float32
        )
        expl = jnp.exp(logits)
        probs = expl / jnp.sum(expl, axis=-1, keepdims=True)
        probs_v[m] = probs
        named = routes_ref[m]
        first = (named[:, 0:1] == expert_ids).astype(jnp.float32)
        second = (named[:, 1:2] == expert_ids).astype(jnp.float32)
        chosen_v[m, 0] = first
        chosen_v[m, 1] = second
        either = first + second
        before = jnp.dot(earlier, either.astype(jnp.bfloat16), preferred_element_type=jnp.float32)
        slot = jnp.where(either > 0.5, before.astype(jnp.int32), -1)
        ids = lax.broadcasted_iota(jnp.int32, (rows, columns), 1)
        for p in range(n_pairs):
            first_expert = first_of(p)
            pick = jnp.zeros((rows, columns), jnp.float32)
            for place, e in enumerate((first_expert, 4 * p + 1 - first_expert)):
                this = expert_ids == e
                at = jnp.sum(jnp.where(this, slot, 0), axis=1, keepdims=True)
                gate = jnp.sum(jnp.where(this, probs, 0.0), axis=1, keepdims=True)
                late = 2 * whole_rows + place * tail_rows + at - whole_rows + m * rest
                there = jnp.where(at < whole_rows, at + place * whole_rows, late)
                there = jnp.where(at < 0, -1, there)
                pick += jnp.where(there == ids, gate, 0.0)
            high = pick.astype(jnp.bfloat16)
            low = (pick - high.astype(jnp.float32)).astype(jnp.bfloat16)
            pick_v[p, m, pl.ds(0, rows)] = high
            pick_v[p, m, pl.ds(rows, rows)] = low
        return carry

    lax.fori_loop(0, micro, route, 0)
    for p in range(n_pairs):

        @pl.when(p != pair)
        def _():
            pick_copy(p).start()

    for t in range(1, n_expert):
        send_first(t)

    def send_near(m):
        if rest and m == 0:
            tail_copy(mate).start()
        if whole_rows:
            main_copy(m, mate).start()

    for m in range(1, micro):
        if whole_rows:
            regroup_main(m)
            for t in range(n_expert):
                j, send = far(t)

                @pl.when(send)
                def _():
                    main_copy(m, j).start()

        send_near(m - 1)
    send_near(micro - 1)

    lax.fori_loop(0, micro * (width // tile), regroup, 0)

    @pl.when(pipe == n_pipe - 1)
    def _():
        top_load.wait()

    def await_slots(m, j):
        if whole_rows:
            main_copy(m, j).wait_recv()
        if rest:

            @pl.when(m == 0)
            def _():
                tail_copy(j).wait_recv()

    def picked(m, j, pick, cols):
        slots = []
        if whole_rows:
            slots += [main_v[m, j, :, cols], mate_main_v[m, j, :, cols]]
        if rest:
            slots += [tail_v[j, :, cols], mate_tail_v[j, :, cols]]
        return jnp.dot(
            pick, jnp.concatenate(slots, axis=0), preferred_element_type=jnp.float32
        )

    def sum_for_others(m):
        def one(t, carry):
            j = jnp.where(odd == 1, n_expert - 1 - t, t)

            @pl.when(summed_here(j))
            def _():
                await_slots(m, j)

                @pl.when(m == 0)
                def _():
                    pick_arrival(j).wait_recv()

                @pl.when(m >= 2)
                def _():
                    term_copy(m - 2, j).wait_send()

                pick = asked_v[j, m]

                def combine(i, inner):
                    cols = columns_of(i)
                    sums_v[lax.rem(m, 2), j, :, cols] = picked(m, j, pick, cols).astype(
                        jnp.bfloat16
                    )
                    return inner

                lax.fori_loop(0, tiles, combine, 0, unroll=True)
                term_copy(m, j).start()

            return carry

        lax.fori_loop(0, n_expert, one, 0)

    offset = lax.broadcasted_iota(jnp.int32, (PACK, 2 * PACK), 1) - 2 * lax.broadcasted_iota(
        jnp.int32, (PACK, 2 * PACK), 0
    )

    def relay(m, q):
        part = pl.ds(pl.multiple_of(q * PACK, PACK), PACK)
        return pltpu.make_async_remote_copy(
            src_ref=out_ref.at[m, part],
            dst_ref=inc_v.at[m, part],
            send_sem=relay_send.at[m, q],
            recv_sem=relay_recv.at[m, q],
            device_id={"pipe": jnp.maximum(pipe - 1, 0)},
            device_id_type=MESH,
        )

    def block(m):
        await_slots(m, expert)
        pick = pick_v[pair, m]

        def combine(i, inner):
            cols = columns_of(i)
            both = picked(m, expert, pick, cols)
            total_v[:, cols] = both[:rows] + both[rows:]
            return inner

        lax.fori_loop(0, tiles, combine, 0, unroll=True)

        def join(p, carry):
            @pl.when(p != pair)
            def _():
                term_arrival(m, p).wait_recv()

                def add(i, inner):
                    cols = columns_of(i)
                    total_v[:, cols] += terms_v[m, p, :, cols].astype(jnp.float32)
                    return inner

                lax.fori_loop(0, tiles, add, 0, unroll=True)

            return carry

        lax.fori_loop(0, n_pairs, join, 0)

        def step(q, inner):
            part = pl.ds(pl.multiple_of(q * PACK, PACK), PACK)

            @pl.when(pipe < n_pipe - 1)
            def _():
                relay(m, q).wait_recv()

            cross = lax.dot_general(
                inc_v[m, part],
                saved_v[m, pl.ds(pl.multiple_of(q * 2 * PACK, 2 * PACK), 2 * PACK)],
                (((1,), (1,)), ((), ())),
                preferred_element_type=jnp.float32,
            )
            probs = probs_v[m, part]
            weighted = jnp.zeros((PACK, experts), jnp.float32)
            for k in range(2):
                dot = jnp.sum(jnp.where(offset == k, cross, 0.0), axis=1, keepdims=True)
                weighted += dot * probs * chosen_v[m, k, part]
            dense = (weighted - probs * jnp.sum(weighted, axis=1, keepdims=True)).astype(jnp.bfloat16)
            dense_v[part] = dense

            def finish(i, innermost):
                cols = pl.ds(pl.multiple_of(i * tile, tile), tile)
                term = jnp.dot(dense, weight_ref[:, cols], preferred_element_type=jnp.float32)
                whole = inc_v[m, part, cols].astype(jnp.float32) + total_v[part, cols] + term
                out_ref[m, part, cols] = whole.astype(jnp.bfloat16)
                return innermost

            lax.fori_loop(0, width // tile, finish, 0, unroll=True)

            @pl.when(pipe > 0)
            def _():
                relay(m, q).start()

            return inner

        lax.fori_loop(0, rows // PACK, step, 0)
        dense = dense_v[...]

        def weigh(i, inner):
            cols = pl.ds(pl.multiple_of(i * chunk, chunk), chunk)
            wpart_v[i] += lax.dot_general(
                dense,
                normed_v[m, :, cols],
                (((0,), (0,)), ((), ())),
                preferred_element_type=jnp.float32,
            )
            return inner

        lax.fori_loop(0, chunks, weigh, 0)

    def turn(m, carry):
        @pl.when(m < micro)
        def _():
            sum_for_others(m)

        @pl.when(m > 0)
        def _():
            block(m - 1)

        return carry

    lax.fori_loop(0, micro + 1, turn, 0)

    def part_copy(distance):
        other, place = member(distance)
        return pltpu.make_async_remote_copy(
            src_ref=wpart_v.at[jnp.minimum(other, chunks - 1)],
            dst_ref=wrecv_v.at[me],
            send_sem=part_send.at[other],
            recv_sem=part_recv.at[me],
            device_id=place,
            device_id_type=MESH,
        ), other

    def part_arrival(distance):
        other, place = member(distance)
        return pltpu.make_async_remote_copy(
            src_ref=wpart_v.at[0],
            dst_ref=wrecv_v.at[other],
            send_sem=part_send.at[other],
            recv_sem=part_recv.at[other],
            device_id=place,
            device_id_type=MESH,
        )

    def sum_copy(distance):
        other, place = member(distance)
        spot = jnp.minimum(me, chunks - 1)
        return pltpu.make_async_remote_copy(
            src_ref=wgrad_ref.at[spot],
            dst_ref=wgrad_ref.at[spot],
            send_sem=sum_send.at[other],
            recv_sem=sum_recv.at[me],
            device_id=place,
            device_id_type=MESH,
        )

    def sum_arrival(distance):
        other, place = member(distance)
        spot = jnp.minimum(other, chunks - 1)
        return pltpu.make_async_remote_copy(
            src_ref=wgrad_ref.at[spot],
            dst_ref=wgrad_ref.at[spot],
            send_sem=sum_send.at[other],
            recv_sem=sum_recv.at[other],
            device_id=place,
            device_id_type=MESH,
        ), other

    for distance in range(1, group):
        copy, other = part_copy(distance)

        @pl.when(other < chunks)
        def _():
            copy.start()

    @pl.when(me < chunks)
    def _():
        total = wpart_v[me]
        for distance in range(1, group):
            part_arrival(distance).wait_recv()
            total += wrecv_v[member(distance)[0]]
        wgrad_ref[me] = total * (1.0 / micro)
        for distance in range(1, group):
            sum_copy(distance).start()

    for distance in range(1, group):
        copy, other = sum_arrival(distance)

        @pl.when(other < chunks)
        def _():
            copy.wait_recv()

    for j in range(n_expert):

        @pl.when((expert != j) & jnp.logical_not(summed_here(j)))
        def _():
            if rest:
                tail_copy(j).wait_send()
            if whole_rows:
                for m in range(micro):
                    main_copy(m, j).wait_send()

        @pl.when(summed_here(j))
        def _():
            for m in range(max(micro - 2, 0), micro):
                term_copy(m, j).wait_send()

    for p in range(n_pairs):

        @pl.when(p != pair)
        def _():
            pick_copy(p).wait_send()

    @pl.when(pipe > 0)
    def _():
        for m in range(micro):
            for q in range(rows // PACK):
                relay(m, q).wait_send()

    for distance in range(1, group):
        copy, other = part_copy(distance)

        @pl.when(other < chunks)
        def _():
            copy.wait_send()

    @pl.when(me < chunks)
    def _():
        for distance in range(1, group):
            sum_copy(distance).wait_send()


def on_device(sizes, normed, saved_out, expert_grads, routes, router_weight, upstream):
    n_pipe, n_expert, n_dp = sizes
    micro, rows, width = normed.shape[1:]
    experts = router_weight.shape[2]
    capacity = expert_grads.shape[5]
    whole_rows = capacity // PACK * PACK
    rest = capacity - whole_rows
    tail_rows = -(-max(rest * micro, 1) // PACK) * PACK
    group = n_expert * n_dp
    chunks = min(group, width // 128)
    chunk = width // chunks
    grads = jnp.swapaxes(expert_grads.reshape(micro, n_expert, capacity, width), 1, 2)
    columns = 2 * (whole_rows + (tail_rows if rest else 0))
    main_shape = (
        (micro, n_expert, whole_rows, width) if whole_rows else (1, 1, PACK, width)
    )
    tail_shape = (n_expert, tail_rows, width) if rest else (1, tail_rows, width)
    n_pairs = n_expert // 2
    any_space = pl.BlockSpec(memory_space=pl.ANY)
    vmem = pl.BlockSpec(memory_space=pltpu.VMEM)
    dma = pltpu.SemaphoreType.DMA
    out, wgrad = pl.pallas_call(
        functools.partial(kernel, sizes),
        out_shape=(
            jax.ShapeDtypeStruct((micro, rows, width), jnp.bfloat16),
            jax.ShapeDtypeStruct((chunks, experts, chunk), jnp.float32),
        ),
        in_specs=[any_space] * 4 + [vmem] * 2,
        out_specs=(vmem, vmem),
        scratch_shapes=[
            pltpu.VMEM((micro, capacity, n_expert, width), jnp.bfloat16),
            pltpu.VMEM(main_shape, jnp.bfloat16),
            pltpu.VMEM(tail_shape, jnp.bfloat16),
            pltpu.VMEM(main_shape, jnp.bfloat16),
            pltpu.VMEM(tail_shape, jnp.bfloat16),
            pltpu.VMEM((2, n_expert, rows, width), jnp.bfloat16),
            pltpu.VMEM((micro, n_pairs, rows, width), jnp.bfloat16),
            pltpu.VMEM((micro, rows, width), jnp.bfloat16),
            pltpu.VMEM((micro, rows, 2, width), jnp.bfloat16),
            pltpu.VMEM((micro, 2 * rows, width), jnp.bfloat16),
            pltpu.VMEM((micro, rows, width), jnp.bfloat16),
            pltpu.VMEM((rows, width), jnp.float32),
            pltpu.VMEM((rows, experts), jnp.bfloat16),
            pltpu.VMEM((n_pairs, micro, 2 * rows, columns), jnp.bfloat16),
            pltpu.VMEM((n_expert, micro, rows, columns), jnp.bfloat16),
            pltpu.VMEM((micro, rows, experts), jnp.float32),
            pltpu.VMEM((micro, 2, rows, experts), jnp.float32),
            pltpu.VMEM((chunks, experts, chunk), jnp.float32),
            pltpu.VMEM((group, experts, chunk), jnp.float32),
            dma((micro,)),
            dma((micro, n_expert)),
            dma((micro, n_expert)),
            dma((n_expert,)),
            dma((n_expert,)),
            dma((n_pairs,)),
            dma((n_expert,)),
            dma((micro, n_expert)),
            dma((micro, n_pairs)),
            dma((2,)),
            dma,
            dma((micro, rows // PACK)),
            dma((micro, rows // PACK)),
            dma((group,)),
            dma((group,)),
            dma((group,)),
            dma((group,)),
        ],
        compiler_params=pltpu.CompilerParams(
            collective_id=0, has_side_effects=True, vmem_limit_bytes=60 * 2**20
        ),
        name="relay",
    )(
        grads,
        normed[0],
        saved_out[0],
        upstream,
        routes[0],
        router_weight[0].T,
    )
    router_grad = jnp.transpose(wgrad, (0, 2, 1)).reshape(width, experts)
    return (out[None], router_grad[None])


def solution(mesh):
    in_specs = (
        P("pipe", None, ("expert", "dp"), None),
        P("pipe", None, ("expert", "dp"), None, None),
        P("pipe", None, "dp", "expert", None, None, None),
        P("pipe", None, ("expert", "dp"), None),
        P("pipe", None, None),
        P(None, ("expert", "dp"), None),
    )
    out_specs = (P("pipe", None, ("expert", "dp"), None), P("pipe", None, None))
    sizes = (mesh.shape["pipe"], mesh.shape["expert"], mesh.shape["dp"])
    return jax.shard_map(
        functools.partial(on_device, sizes),
        mesh=mesh,
        in_specs=in_specs,
        out_specs=out_specs,
        check_vma=False,
    )
```

```python
import functools

import jax
import jax.numpy as jnp
from jax import lax
from jax.experimental import pallas as pl
from jax.experimental.pallas import tpu as pltpu
from jax.sharding import PartitionSpec as P

MESH = pl.DeviceIdType.MESH
PACK = 16


def kernel(
    sizes,
    grads_ref,
    normed_ref,
    saved_ref,
    upstream_ref,
    routes_ref,
    weight_ref,
    out_ref,
    wgrad_ref,
    grads_v,
    main_v,
    tail_v,
    mate_main_v,
    mate_tail_v,
    sums_v,
    terms_v,
    normed_v,
    pairs_v,
    saved_v,
    inc_v,
    out_v,
    total_v,
    dense_v,
    pick_v,
    asked_v,
    probs_v,
    chosen_v,
    wpart_v,
    wrecv_v,
    grads_sem,
    main_send,
    main_recv,
    tail_send,
    tail_recv,
    pick_send,
    pick_recv,
    term_send,
    term_recv,
    load_sem,
    top_sem,
    relay_send,
    relay_recv,
    out_sem,
    part_send,
    part_recv,
    sum_send,
    sum_recv,
):
    n_pipe, n_expert, n_dp = sizes
    micro, rows, width = normed_v.shape
    experts = weight_ref.shape[0]
    capacity = grads_ref.shape[1]
    whole_rows = capacity // PACK * PACK
    rest = capacity - whole_rows
    tail_rows = tail_v.shape[1]
    columns = pick_v.shape[3]
    n_pairs = n_expert // 2
    group = n_expert * n_dp
    chunks, _, chunk = wpart_v.shape
    tile = min(width, 512)
    pipe = lax.axis_index("pipe")
    expert = lax.axis_index("expert")
    dp = lax.axis_index("dp")
    me = expert * n_dp + dp
    pair = expert // 2
    odd = lax.rem(expert, 2)
    mate = expert + 1 - 2 * odd

    def summed_here(j):
        return ((odd == 1) & (j > expert)) | ((odd == 0) & (j < expert))

    def member(distance):
        other = lax.rem(me + distance, group)
        return other, {"expert": other // n_dp, "dp": lax.rem(other, n_dp)}

    barrier = pltpu.get_barrier_semaphore()
    for distance in range(1, group):
        _, place = member(distance)
        pl.semaphore_signal(barrier, inc=1, device_id=place, device_id_type=MESH)

    @pl.when(pipe > 0)
    def _():
        pl.semaphore_signal(barrier, inc=1, device_id={"pipe": pipe - 1}, device_id_type=MESH)

    @pl.when(pipe < n_pipe - 1)
    def _():
        pl.semaphore_signal(barrier, inc=1, device_id={"pipe": pipe + 1}, device_id_type=MESH)

    def grads_load(m):
        return pltpu.make_async_copy(grads_ref.at[m], grads_v.at[m], grads_sem.at[m])

    for m in range(micro):
        grads_load(m).start()
    loads = [
        pltpu.make_async_copy(normed_ref, normed_v, load_sem.at[0]),
        pltpu.make_async_copy(saved_ref, pairs_v, load_sem.at[1]),
    ]
    top_load = pltpu.make_async_copy(upstream_ref, inc_v, top_sem)
    for load in loads:
        load.start()

    @pl.when(pipe == n_pipe - 1)
    def _():
        top_load.start()

    def tail_copy(j):
        return pltpu.make_async_remote_copy(
            src_ref=tail_v.at[j],
            dst_ref=mate_tail_v.at[j],
            send_sem=tail_send.at[j],
            recv_sem=tail_recv.at[j],
            device_id={"expert": mate},
            device_id_type=MESH,
        )

    def main_copy(m, j):
        return pltpu.make_async_remote_copy(
            src_ref=main_v.at[m, j],
            dst_ref=mate_main_v.at[m, j],
            send_sem=main_send.at[m, j],
            recv_sem=main_recv.at[m, j],
            device_id={"expert": mate},
            device_id_type=MESH,
        )

    def first_of(p):
        return jnp.where(p == pair, expert, jnp.where(p < pair, 2 * p + 1, 2 * p))

    def pick_copy(p):
        return pltpu.make_async_remote_copy(
            src_ref=pick_v.at[p, :, pl.ds(0, rows)],
            dst_ref=asked_v.at[expert],
            send_sem=pick_send.at[p],
            recv_sem=pick_recv.at[expert],
            device_id={"expert": first_of(p)},
            device_id_type=MESH,
        )

    def pick_arrival(j):
        return pltpu.make_async_remote_copy(
            src_ref=pick_v.at[0, :, pl.ds(0, rows)],
            dst_ref=asked_v.at[j],
            send_sem=pick_send.at[0],
            recv_sem=pick_recv.at[j],
            device_id={"expert": j},
            device_id_type=MESH,
        )

    def term_copy(m, j):
        return pltpu.make_async_remote_copy(
            src_ref=sums_v.at[lax.rem(m, 2), j],
            dst_ref=terms_v.at[m, pair],
            send_sem=term_send.at[m, j],
            recv_sem=term_recv.at[m, pair],
            device_id={"expert": j},
            device_id_type=MESH,
        )

    def term_arrival(m, p):
        return pltpu.make_async_remote_copy(
            src_ref=sums_v.at[0, 0],
            dst_ref=terms_v.at[m, p],
            send_sem=term_send.at[m, 0],
            recv_sem=term_recv.at[m, p],
            device_id={"expert": first_of(p)},
            device_id_type=MESH,
        )

    def far(t):
        j = jnp.where(odd == 1, t, n_expert - 1 - t)
        return j, (j != expert) & (j != mate) & jnp.logical_not(summed_here(j))

    tiles = width // tile

    def columns_of(i):
        return pl.ds(pl.multiple_of(i * tile, tile), tile)

    if rest:
        shape = (n_expert * tail_rows, micro * rest * n_expert)
        row, col = (lax.broadcasted_iota(jnp.int32, shape, axis) for axis in (0, 1))
        tail_order = (
            col == lax.rem(row, tail_rows) * n_expert + lax.div(row, tail_rows)
        ).astype(jnp.bfloat16)
    if whole_rows:
        shape = (n_expert * whole_rows, n_expert * whole_rows)
        row, col = (lax.broadcasted_iota(jnp.int32, shape, axis) for axis in (0, 1))
        main_order = (
            col == lax.rem(row, whole_rows) * n_expert + lax.div(row, whole_rows)
        ).astype(jnp.bfloat16)

    def regroup_tail(i, carry):
        cols = columns_of(i)
        slots = jnp.concatenate(
            [
                grads_v[m, whole_rows:, :, cols].reshape(rest * n_expert, tile)
                for m in range(micro)
            ],
            axis=0,
        )
        ordered = jnp.dot(tail_order, slots, preferred_element_type=jnp.float32)
        tail_v[:, :, cols] = ordered.astype(jnp.bfloat16).reshape(n_expert, tail_rows, tile)
        return carry

    def regroup_main(m):
        def regroup(i, carry):
            cols = columns_of(i)
            slots = grads_v[m, :whole_rows, :, cols].reshape(whole_rows * n_expert, tile)
            ordered = jnp.dot(main_order, slots, preferred_element_type=jnp.float32)
            main_v[m, :, :, cols] = ordered.astype(jnp.bfloat16).reshape(
                n_expert, whole_rows, tile
            )
            return carry

        lax.fori_loop(0, tiles, regroup, 0, unroll=4)

    def send_first(t):
        j, send = far(t)

        @pl.when(send)
        def _():
            main_copy(0, j).start()

    def send_first_tail(t):
        j, send = far(t)

        @pl.when(send)
        def _():
            tail_copy(j).start()

    grads_load(0).wait()
    if whole_rows:
        regroup_main(0)
    pl.semaphore_wait(
        barrier,
        group - 1 + jnp.where(pipe > 0, 1, 0) + jnp.where(pipe < n_pipe - 1, 1, 0),
    )
    if whole_rows:
        send_first(0)
    for m in range(1, micro):
        grads_load(m).wait()
    if rest:
        lax.fori_loop(0, tiles, regroup_tail, 0, unroll=4)
        send_first_tail(0)

    wpart_v[...] = jnp.zeros_like(wpart_v)
    for load in loads:
        load.wait()

    weight = weight_ref[...]
    earlier = (
        lax.broadcasted_iota(jnp.int32, (rows, rows), 0)
        > lax.broadcasted_iota(jnp.int32, (rows, rows), 1)
    ).astype(jnp.bfloat16)
    same = lax.broadcasted_iota(jnp.int32, (rows, rows), 0) == lax.broadcasted_iota(
        jnp.int32, (rows, rows), 1
    )
    expert_ids = lax.broadcasted_iota(jnp.int32, (rows, experts), 1)

    def regroup(i, carry):
        m, cols = i // (width // tile), pl.ds(pl.multiple_of(lax.rem(i, width // tile) * tile, tile), tile)
        saved_v[m, :, cols] = pairs_v[m, :, :, cols].reshape(2 * rows, tile)
        return carry

    def route(m, carry):
        logits = lax.dot_general(
            normed_v[m], weight, (((1,), (1,)), ((), ())), preferred_element_type=jnp.float32
        )
        expl = jnp.exp(logits)
        probs = expl / jnp.sum(expl, axis=-1, keepdims=True)
        probs_v[m] = probs
        named = [
            jnp.sum(jnp.where(same, routes_ref[m, k : k + 1, :], 0), axis=1, keepdims=True)
            for k in range(2)
        ]
        first = (named[0] == expert_ids).astype(jnp.float32)
        second = (named[1] == expert_ids).astype(jnp.float32)
        chosen_v[m, 0] = first
        chosen_v[m, 1] = second
        either = first + second
        before = jnp.dot(earlier, either.astype(jnp.bfloat16), preferred_element_type=jnp.float32)
        slot = jnp.where(either > 0.5, before.astype(jnp.int32), -1)
        ids = lax.broadcasted_iota(jnp.int32, (rows, columns), 1)
        for p in range(n_pairs):
            first_expert = first_of(p)
            pick = jnp.zeros((rows, columns), jnp.float32)
            for place, e in enumerate((first_expert, 4 * p + 1 - first_expert)):
                this = expert_ids == e
                at = jnp.sum(jnp.where(this, slot, 0), axis=1, keepdims=True)
                gate = jnp.sum(jnp.where(this, probs, 0.0), axis=1, keepdims=True)
                late = 2 * whole_rows + place * tail_rows + at - whole_rows + m * rest
                there = jnp.where(at < whole_rows, at + place * whole_rows, late)
                there = jnp.where(at < 0, -1, there)
                pick += jnp.where(there == ids, gate, 0.0)
            high = pick.astype(jnp.bfloat16)
            low = (pick - high.astype(jnp.float32)).astype(jnp.bfloat16)
            pick_v[p, m, pl.ds(0, rows)] = high
            pick_v[p, m, pl.ds(rows, rows)] = low
        return carry

    lax.fori_loop(0, micro, route, 0)
    for p in range(n_pairs):

        @pl.when(p != pair)
        def _():
            pick_copy(p).start()

    for t in range(1, n_expert):
        if whole_rows:
            send_first(t)
        if rest:
            send_first_tail(t)

    def send_near(m):
        if rest and m == 0:
            tail_copy(mate).start()
        if whole_rows:
            main_copy(m, mate).start()

    for m in range(1, micro):
        if whole_rows:
            regroup_main(m)
            for t in range(n_expert):
                j, send = far(t)

                @pl.when(send)
                def _():
                    main_copy(m, j).start()

        send_near(m - 1)
    send_near(micro - 1)

    lax.fori_loop(0, micro * (width // tile), regroup, 0)

    @pl.when(pipe == n_pipe - 1)
    def _():
        top_load.wait()

    def out_copy(m, q):
        part = pl.ds(pl.multiple_of(q * PACK, PACK), PACK)
        return pltpu.make_async_copy(
            out_v.at[m, part], out_ref.at[m, part], out_sem.at[m, q]
        )

    def await_slots(m, j):
        if whole_rows:
            main_copy(m, j).wait_recv()
        if rest:

            @pl.when(m == 0)
            def _():
                tail_copy(j).wait_recv()

    def picked(m, j, pick, cols):
        slots = []
        if whole_rows:
            slots += [main_v[m, j, :, cols], mate_main_v[m, j, :, cols]]
        if rest:
            slots += [tail_v[j, :, cols], mate_tail_v[j, :, cols]]
        return jnp.dot(
            pick, jnp.concatenate(slots, axis=0), preferred_element_type=jnp.float32
        )

    def sum_for_others(m):
        def one(t, carry):
            j = jnp.where(odd == 1, n_expert - 1 - t, t)

            @pl.when(summed_here(j))
            def _():
                await_slots(m, j)

                @pl.when(m == 0)
                def _():
                    pick_arrival(j).wait_recv()

                @pl.when(m >= 2)
                def _():
                    term_copy(m - 2, j).wait_send()

                pick = asked_v[j, m]

                def combine(i, inner):
                    cols = columns_of(i)
                    sums_v[lax.rem(m, 2), j, :, cols] = picked(m, j, pick, cols).astype(
                        jnp.bfloat16
                    )
                    return inner

                lax.fori_loop(0, tiles, combine, 0, unroll=True)
                term_copy(m, j).start()

            return carry

        lax.fori_loop(0, n_expert, one, 0)

    offset = lax.broadcasted_iota(jnp.int32, (PACK, 2 * PACK), 1) - 2 * lax.broadcasted_iota(
        jnp.int32, (PACK, 2 * PACK), 0
    )

    def relay(m, q):
        part = pl.ds(pl.multiple_of(q * PACK, PACK), PACK)
        return pltpu.make_async_remote_copy(
            src_ref=out_v.at[m, part],
            dst_ref=inc_v.at[m, part],
            send_sem=relay_send.at[m, q],
            recv_sem=relay_recv.at[m, q],
            device_id={"pipe": jnp.maximum(pipe - 1, 0)},
            device_id_type=MESH,
        )

    def block(m):
        await_slots(m, expert)
        pick = pick_v[pair, m]

        def combine(i, inner):
            cols = columns_of(i)
            both = picked(m, expert, pick, cols)
            total_v[:, cols] = both[:rows] + both[rows:]
            return inner

        lax.fori_loop(0, tiles, combine, 0, unroll=True)

        def join(p, carry):
            @pl.when(p != pair)
            def _():
                term_arrival(m, p).wait_recv()

                def add(i, inner):
                    cols = columns_of(i)
                    total_v[:, cols] += terms_v[m, p, :, cols].astype(jnp.float32)
                    return inner

                lax.fori_loop(0, tiles, add, 0, unroll=True)

            return carry

        lax.fori_loop(0, n_pairs, join, 0)

        def step(q, inner):
            part = pl.ds(pl.multiple_of(q * PACK, PACK), PACK)

            @pl.when(pipe < n_pipe - 1)
            def _():
                relay(m, q).wait_recv()

            cross = lax.dot_general(
                inc_v[m, part],
                saved_v[m, pl.ds(pl.multiple_of(q * 2 * PACK, 2 * PACK), 2 * PACK)],
                (((1,), (1,)), ((), ())),
                preferred_element_type=jnp.float32,
            )
            probs = probs_v[m, part]
            weighted = jnp.zeros((PACK, experts), jnp.float32)
            for k in range(2):
                dot = jnp.sum(jnp.where(offset == k, cross, 0.0), axis=1, keepdims=True)
                weighted += dot * probs * chosen_v[m, k, part]
            dense = (weighted - probs * jnp.sum(weighted, axis=1, keepdims=True)).astype(jnp.bfloat16)
            dense_v[part] = dense

            def finish(i, innermost):
                cols = pl.ds(pl.multiple_of(i * tile, tile), tile)
                term = jnp.dot(dense, weight_ref[:, cols], preferred_element_type=jnp.float32)
                whole = inc_v[m, part, cols].astype(jnp.float32) + total_v[part, cols] + term
                out_v[m, part, cols] = whole.astype(jnp.bfloat16)
                return innermost

            lax.fori_loop(0, width // tile, finish, 0, unroll=True)

            @pl.when(pipe > 0)
            def _():
                relay(m, q).start()

            out_copy(m, q).start()
            return inner

        lax.fori_loop(0, rows // PACK, step, 0)
        dense = dense_v[...]

        def weigh(i, inner):
            cols = pl.ds(pl.multiple_of(i * chunk, chunk), chunk)
            wpart_v[i] += lax.dot_general(
                dense,
                normed_v[m, :, cols],
                (((0,), (0,)), ((), ())),
                preferred_element_type=jnp.float32,
            )
            return inner

        lax.fori_loop(0, chunks, weigh, 0, unroll=8)

    def turn(m, carry):
        @pl.when(m < micro)
        def _():
            sum_for_others(m)

        @pl.when(m > 0)
        def _():
            block(m - 1)

        return carry

    lax.fori_loop(0, micro + 1, turn, 0)

    def part_copy(distance):
        other, place = member(distance)
        return pltpu.make_async_remote_copy(
            src_ref=wpart_v.at[jnp.minimum(other, chunks - 1)],
            dst_ref=wrecv_v.at[me],
            send_sem=part_send.at[other],
            recv_sem=part_recv.at[me],
            device_id=place,
            device_id_type=MESH,
        ), other

    def part_arrival(distance):
        other, place = member(distance)
        return pltpu.make_async_remote_copy(
            src_ref=wpart_v.at[0],
            dst_ref=wrecv_v.at[other],
            send_sem=part_send.at[other],
            recv_sem=part_recv.at[other],
            device_id=place,
            device_id_type=MESH,
        )

    def sum_copy(distance):
        other, place = member(distance)
        spot = jnp.minimum(me, chunks - 1)
        return pltpu.make_async_remote_copy(
            src_ref=wgrad_ref.at[spot],
            dst_ref=wgrad_ref.at[spot],
            send_sem=sum_send.at[other],
            recv_sem=sum_recv.at[me],
            device_id=place,
            device_id_type=MESH,
        )

    def sum_arrival(distance):
        other, place = member(distance)
        spot = jnp.minimum(other, chunks - 1)
        return pltpu.make_async_remote_copy(
            src_ref=wgrad_ref.at[spot],
            dst_ref=wgrad_ref.at[spot],
            send_sem=sum_send.at[other],
            recv_sem=sum_recv.at[other],
            device_id=place,
            device_id_type=MESH,
        ), other

    for distance in range(1, group):
        copy, other = part_copy(distance)

        @pl.when(other < chunks)
        def _():
            copy.start()

    @pl.when(me < chunks)
    def _():
        total = wpart_v[me]
        for distance in range(1, group):
            part_arrival(distance).wait_recv()
            total += wrecv_v[member(distance)[0]]
        wgrad_ref[me] = total * (1.0 / micro)
        for distance in range(1, group):
            sum_copy(distance).start()

    for distance in range(1, group):
        copy, other = sum_arrival(distance)

        @pl.when(other < chunks)
        def _():
            copy.wait_recv()

    for j in range(n_expert):

        @pl.when((expert != j) & jnp.logical_not(summed_here(j)))
        def _():
            if rest:
                tail_copy(j).wait_send()
            if whole_rows:
                for m in range(micro):
                    main_copy(m, j).wait_send()

        @pl.when(summed_here(j))
        def _():
            for m in range(max(micro - 2, 0), micro):
                term_copy(m, j).wait_send()

    for m in range(micro):
        for q in range(rows // PACK):
            out_copy(m, q).wait()

    for p in range(n_pairs):

        @pl.when(p != pair)
        def _():
            pick_copy(p).wait_send()

    @pl.when(pipe > 0)
    def _():
        for m in range(micro):
            for q in range(rows // PACK):
                relay(m, q).wait_send()

    for distance in range(1, group):
        copy, other = part_copy(distance)

        @pl.when(other < chunks)
        def _():
            copy.wait_send()

    @pl.when(me < chunks)
    def _():
        for distance in range(1, group):
            sum_copy(distance).wait_send()


def on_device(sizes, normed, saved_out, expert_grads, routes, router_weight, upstream):
    n_pipe, n_expert, n_dp = sizes
    micro, rows, width = normed.shape[1:]
    experts = router_weight.shape[2]
    capacity = expert_grads.shape[5]
    whole_rows = capacity // PACK * PACK
    rest = capacity - whole_rows
    tail_rows = -(-max(rest * micro, 1) // PACK) * PACK
    group = n_expert * n_dp
    chunks = min(group, width // 128)
    chunk = width // chunks
    grads = jnp.swapaxes(expert_grads.reshape(micro, n_expert, capacity, width), 1, 2)
    columns = 2 * (whole_rows + (tail_rows if rest else 0))
    main_shape = (
        (micro, n_expert, whole_rows, width) if whole_rows else (1, 1, PACK, width)
    )
    tail_shape = (n_expert, tail_rows, width) if rest else (1, tail_rows, width)
    n_pairs = n_expert // 2
    any_space = pl.BlockSpec(memory_space=pl.ANY)
    vmem = pl.BlockSpec(memory_space=pltpu.VMEM)
    dma = pltpu.SemaphoreType.DMA
    out, wgrad = pl.pallas_call(
        functools.partial(kernel, sizes),
        out_shape=(
            jax.ShapeDtypeStruct((micro, rows, width), jnp.bfloat16),
            jax.ShapeDtypeStruct((chunks, experts, chunk), jnp.float32),
        ),
        in_specs=[any_space] * 4 + [vmem] * 2,
        out_specs=(any_space, vmem),
        scratch_shapes=[
            pltpu.VMEM((micro, capacity, n_expert, width), jnp.bfloat16),
            pltpu.VMEM(main_shape, jnp.bfloat16),
            pltpu.VMEM(tail_shape, jnp.bfloat16),
            pltpu.VMEM(main_shape, jnp.bfloat16),
            pltpu.VMEM(tail_shape, jnp.bfloat16),
            pltpu.VMEM((2, n_expert, rows, width), jnp.bfloat16),
            pltpu.VMEM((micro, n_pairs, rows, width), jnp.bfloat16),
            pltpu.VMEM((micro, rows, width), jnp.bfloat16),
            pltpu.VMEM((micro, rows, 2, width), jnp.bfloat16),
            pltpu.VMEM((micro, 2 * rows, width), jnp.bfloat16),
            pltpu.VMEM((micro, rows, width), jnp.bfloat16),
            pltpu.VMEM((micro, rows, width), jnp.bfloat16),
            pltpu.VMEM((rows, width), jnp.float32),
            pltpu.VMEM((rows, experts), jnp.bfloat16),
            pltpu.VMEM((n_pairs, micro, 2 * rows, columns), jnp.bfloat16),
            pltpu.VMEM((n_expert, micro, rows, columns), jnp.bfloat16),
            pltpu.VMEM((micro, rows, experts), jnp.float32),
            pltpu.VMEM((micro, 2, rows, experts), jnp.float32),
            pltpu.VMEM((chunks, experts, chunk), jnp.float32),
            pltpu.VMEM((group, experts, chunk), jnp.float32),
            dma((micro,)),
            dma((micro, n_expert)),
            dma((micro, n_expert)),
            dma((n_expert,)),
            dma((n_expert,)),
            dma((n_pairs,)),
            dma((n_expert,)),
            dma((micro, n_expert)),
            dma((micro, n_pairs)),
            dma((2,)),
            dma,
            dma((micro, rows // PACK)),
            dma((micro, rows // PACK)),
            dma((micro, rows // PACK)),
            dma((group,)),
            dma((group,)),
            dma((group,)),
            dma((group,)),
        ],
        compiler_params=pltpu.CompilerParams(
            collective_id=0, has_side_effects=True, vmem_limit_bytes=60 * 2**20
        ),
        name="relay",
    )(
        grads,
        normed[0],
        saved_out[0],
        upstream,
        jnp.swapaxes(routes[0], 1, 2),
        router_weight[0].T,
    )
    router_grad = jnp.transpose(wgrad, (0, 2, 1)).reshape(width, experts)
    return (out[None], router_grad[None])


def solution(mesh):
    in_specs = (
        P("pipe", None, ("expert", "dp"), None),
        P("pipe", None, ("expert", "dp"), None, None),
        P("pipe", None, "dp", "expert", None, None, None),
        P("pipe", None, ("expert", "dp"), None),
        P("pipe", None, None),
        P(None, ("expert", "dp"), None),
    )
    out_specs = (P("pipe", None, ("expert", "dp"), None), P("pipe", None, None))
    sizes = (mesh.shape["pipe"], mesh.shape["expert"], mesh.shape["dp"])
    return jax.shard_map(
        functools.partial(on_device, sizes),
        mesh=mesh,
        in_specs=in_specs,
        out_specs=out_specs,
        check_vma=False,
    )
```

```python
import functools

import jax
import jax.numpy as jnp
from jax import lax
from jax.experimental import pallas as pl
from jax.experimental.pallas import tpu as pltpu
from jax.sharding import PartitionSpec as P

MESH = pl.DeviceIdType.MESH
PACK = 16


def kernel(
    sizes,
    grads_ref,
    normed_ref,
    saved_ref,
    upstream_ref,
    routes_ref,
    weight_ref,
    out_ref,
    wgrad_ref,
    routes_v,
    weight_v,
    grads_v,
    main_v,
    tail_v,
    mate_main_v,
    mate_tail_v,
    sums_v,
    terms_v,
    normed_v,
    pairs_v,
    saved_v,
    inc_v,
    out_v,
    total_v,
    dense_v,
    pick_v,
    asked_v,
    probs_v,
    chosen_v,
    wpart_v,
    wrecv_v,
    grads_sem,
    main_send,
    main_recv,
    tail_send,
    tail_recv,
    pick_send,
    pick_recv,
    term_send,
    term_recv,
    load_sem,
    top_sem,
    relay_send,
    relay_recv,
    out_sem,
    part_send,
    part_recv,
    sum_send,
    sum_recv,
):
    n_pipe, n_expert, n_dp = sizes
    micro, rows, width = normed_v.shape
    experts = weight_ref.shape[0]
    capacity = grads_ref.shape[1]
    whole_rows = capacity // PACK * PACK
    rest = capacity - whole_rows
    tail_rows = tail_v.shape[1]
    columns = pick_v.shape[3]
    n_pairs = n_expert // 2
    group = n_expert * n_dp
    chunks, _, chunk = wpart_v.shape
    tile = min(width, 512)
    pipe = lax.axis_index("pipe")
    expert = lax.axis_index("expert")
    dp = lax.axis_index("dp")
    me = expert * n_dp + dp
    pair = expert // 2
    odd = lax.rem(expert, 2)
    mate = expert + 1 - 2 * odd

    def summed_here(j):
        return ((odd == 1) & (j > expert)) | ((odd == 0) & (j < expert))

    def member(distance):
        other = lax.rem(me + distance, group)
        return other, {"expert": other // n_dp, "dp": lax.rem(other, n_dp)}

    barrier = pltpu.get_barrier_semaphore()
    for distance in range(1, group):
        _, place = member(distance)
        pl.semaphore_signal(barrier, inc=1, device_id=place, device_id_type=MESH)

    @pl.when(pipe > 0)
    def _():
        pl.semaphore_signal(barrier, inc=1, device_id={"pipe": pipe - 1}, device_id_type=MESH)

    @pl.when(pipe < n_pipe - 1)
    def _():
        pl.semaphore_signal(barrier, inc=1, device_id={"pipe": pipe + 1}, device_id_type=MESH)

    def grads_load(m):
        return pltpu.make_async_copy(grads_ref.at[m], grads_v.at[m], grads_sem.at[m])

    for m in range(micro):
        grads_load(m).start()
    loads = [
        pltpu.make_async_copy(normed_ref, normed_v, load_sem.at[0]),
        pltpu.make_async_copy(saved_ref, pairs_v, load_sem.at[1]),
        pltpu.make_async_copy(routes_ref, routes_v, load_sem.at[2]),
        pltpu.make_async_copy(weight_ref, weight_v, load_sem.at[3]),
    ]
    top_load = pltpu.make_async_copy(upstream_ref, inc_v, top_sem)
    for load in loads:
        load.start()

    @pl.when(pipe == n_pipe - 1)
    def _():
        top_load.start()

    def tail_copy(j):
        return pltpu.make_async_remote_copy(
            src_ref=tail_v.at[j],
            dst_ref=mate_tail_v.at[j],
            send_sem=tail_send.at[j],
            recv_sem=tail_recv.at[j],
            device_id={"expert": mate},
            device_id_type=MESH,
        )

    def main_copy(m, j):
        return pltpu.make_async_remote_copy(
            src_ref=main_v.at[m, j],
            dst_ref=mate_main_v.at[m, j],
            send_sem=main_send.at[m, j],
            recv_sem=main_recv.at[m, j],
            device_id={"expert": mate},
            device_id_type=MESH,
        )

    def first_of(p):
        return jnp.where(p == pair, expert, jnp.where(p < pair, 2 * p + 1, 2 * p))

    def pick_copy(p):
        return pltpu.make_async_remote_copy(
            src_ref=pick_v.at[p, :, pl.ds(0, rows)],
            dst_ref=asked_v.at[expert],
            send_sem=pick_send.at[p],
            recv_sem=pick_recv.at[expert],
            device_id={"expert": first_of(p)},
            device_id_type=MESH,
        )

    def pick_arrival(j):
        return pltpu.make_async_remote_copy(
            src_ref=pick_v.at[0, :, pl.ds(0, rows)],
            dst_ref=asked_v.at[j],
            send_sem=pick_send.at[0],
            recv_sem=pick_recv.at[j],
            device_id={"expert": j},
            device_id_type=MESH,
        )

    def term_copy(m, j):
        return pltpu.make_async_remote_copy(
            src_ref=sums_v.at[lax.rem(m, 2), j],
            dst_ref=terms_v.at[m, pair],
            send_sem=term_send.at[m, j],
            recv_sem=term_recv.at[m, pair],
            device_id={"expert": j},
            device_id_type=MESH,
        )

    def term_arrival(m, p):
        return pltpu.make_async_remote_copy(
            src_ref=sums_v.at[0, 0],
            dst_ref=terms_v.at[m, p],
            send_sem=term_send.at[m, 0],
            recv_sem=term_recv.at[m, p],
            device_id={"expert": first_of(p)},
            device_id_type=MESH,
        )

    def far(t):
        j = jnp.where(odd == 1, t, n_expert - 1 - t)
        return j, (j != expert) & (j != mate) & jnp.logical_not(summed_here(j))

    tiles = width // tile

    def columns_of(i):
        return pl.ds(pl.multiple_of(i * tile, tile), tile)

    if rest:
        shape = (n_expert * tail_rows, micro * rest * n_expert)
        row, col = (lax.broadcasted_iota(jnp.int32, shape, axis) for axis in (0, 1))
        tail_order = (
            col == lax.rem(row, tail_rows) * n_expert + lax.div(row, tail_rows)
        ).astype(jnp.bfloat16)
    if whole_rows:
        shape = (n_expert * whole_rows, n_expert * whole_rows)
        row, col = (lax.broadcasted_iota(jnp.int32, shape, axis) for axis in (0, 1))
        main_order = (
            col == lax.rem(row, whole_rows) * n_expert + lax.div(row, whole_rows)
        ).astype(jnp.bfloat16)

    def regroup_tail(i, carry):
        cols = columns_of(i)
        slots = jnp.concatenate(
            [
                grads_v[m, whole_rows:, :, cols].reshape(rest * n_expert, tile)
                for m in range(micro)
            ],
            axis=0,
        )
        ordered = jnp.dot(tail_order, slots, preferred_element_type=jnp.float32)
        tail_v[:, :, cols] = ordered.astype(jnp.bfloat16).reshape(n_expert, tail_rows, tile)
        return carry

    def regroup_main(m):
        def regroup(i, carry):
            cols = columns_of(i)
            slots = grads_v[m, :whole_rows, :, cols].reshape(whole_rows * n_expert, tile)
            ordered = jnp.dot(main_order, slots, preferred_element_type=jnp.float32)
            main_v[m, :, :, cols] = ordered.astype(jnp.bfloat16).reshape(
                n_expert, whole_rows, tile
            )
            return carry

        lax.fori_loop(0, tiles, regroup, 0, unroll=4)

    def send_first(t):
        j, send = far(t)

        @pl.when(send)
        def _():
            main_copy(0, j).start()

    def send_first_tail(t):
        j, send = far(t)

        @pl.when(send)
        def _():
            tail_copy(j).start()

    grads_load(0).wait()
    if whole_rows:
        regroup_main(0)
    pl.semaphore_wait(
        barrier,
        group - 1 + jnp.where(pipe > 0, 1, 0) + jnp.where(pipe < n_pipe - 1, 1, 0),
    )
    if whole_rows:
        send_first(0)
    for m in range(1, micro):
        grads_load(m).wait()
    if rest:
        lax.fori_loop(0, tiles, regroup_tail, 0, unroll=4)
        send_first_tail(0)

    wpart_v[...] = jnp.zeros_like(wpart_v)
    for load in loads:
        load.wait()

    weight = weight_v[...]
    earlier = (
        lax.broadcasted_iota(jnp.int32, (rows, rows), 0)
        > lax.broadcasted_iota(jnp.int32, (rows, rows), 1)
    ).astype(jnp.bfloat16)
    same = lax.broadcasted_iota(jnp.int32, (rows, rows), 0) == lax.broadcasted_iota(
        jnp.int32, (rows, rows), 1
    )
    expert_ids = lax.broadcasted_iota(jnp.int32, (rows, experts), 1)

    def regroup(i, carry):
        m, cols = i // (width // tile), pl.ds(pl.multiple_of(lax.rem(i, width // tile) * tile, tile), tile)
        saved_v[m, :, cols] = pairs_v[m, :, :, cols].reshape(2 * rows, tile)
        return carry

    def route(m, carry):
        logits = lax.dot_general(
            normed_v[m], weight, (((1,), (1,)), ((), ())), preferred_element_type=jnp.float32
        )
        expl = jnp.exp(logits)
        probs = expl / jnp.sum(expl, axis=-1, keepdims=True)
        probs_v[m] = probs
        named = [
            jnp.sum(jnp.where(same, routes_v[m, k : k + 1, :], 0), axis=1, keepdims=True)
            for k in range(2)
        ]
        first = (named[0] == expert_ids).astype(jnp.float32)
        second = (named[1] == expert_ids).astype(jnp.float32)
        chosen_v[m, 0] = first
        chosen_v[m, 1] = second
        either = first + second
        before = jnp.dot(earlier, either.astype(jnp.bfloat16), preferred_element_type=jnp.float32)
        slot = jnp.where(either > 0.5, before.astype(jnp.int32), -1)
        ids = lax.broadcasted_iota(jnp.int32, (rows, columns), 1)
        for p in range(n_pairs):
            first_expert = first_of(p)
            pick = jnp.zeros((rows, columns), jnp.float32)
            for place, e in enumerate((first_expert, 4 * p + 1 - first_expert)):
                this = expert_ids == e
                at = jnp.sum(jnp.where(this, slot, 0), axis=1, keepdims=True)
                gate = jnp.sum(jnp.where(this, probs, 0.0), axis=1, keepdims=True)
                late = 2 * whole_rows + place * tail_rows + at - whole_rows + m * rest
                there = jnp.where(at < whole_rows, at + place * whole_rows, late)
                there = jnp.where(at < 0, -1, there)
                pick += jnp.where(there == ids, gate, 0.0)
            high = pick.astype(jnp.bfloat16)
            low = (pick - high.astype(jnp.float32)).astype(jnp.bfloat16)
            pick_v[p, m, pl.ds(0, rows)] = high
            pick_v[p, m, pl.ds(rows, rows)] = low
        return carry

    lax.fori_loop(0, micro, route, 0)
    for p in range(n_pairs):

        @pl.when(p != pair)
        def _():
            pick_copy(p).start()

    for t in range(1, n_expert):
        if whole_rows:
            send_first(t)
        if rest:
            send_first_tail(t)

    def send_near(m):
        if rest and m == 0:
            tail_copy(mate).start()
        if whole_rows:
            main_copy(m, mate).start()

    for m in range(1, micro):
        if whole_rows:
            regroup_main(m)
            for t in range(n_expert):
                j, send = far(t)

                @pl.when(send)
                def _():
                    main_copy(m, j).start()

        send_near(m - 1)
    send_near(micro - 1)

    lax.fori_loop(0, micro * (width // tile), regroup, 0)

    @pl.when(pipe == n_pipe - 1)
    def _():
        top_load.wait()

    def out_copy(m, q):
        part = pl.ds(pl.multiple_of(q * PACK, PACK), PACK)
        return pltpu.make_async_copy(
            out_v.at[m, part], out_ref.at[m, part], out_sem.at[m, q]
        )

    def await_slots(m, j):
        if whole_rows:
            main_copy(m, j).wait_recv()
        if rest:

            @pl.when(m == 0)
            def _():
                tail_copy(j).wait_recv()

    def picked(m, j, pick, cols):
        slots = []
        if whole_rows:
            slots += [main_v[m, j, :, cols], mate_main_v[m, j, :, cols]]
        if rest:
            slots += [tail_v[j, :, cols], mate_tail_v[j, :, cols]]
        return jnp.dot(
            pick, jnp.concatenate(slots, axis=0), preferred_element_type=jnp.float32
        )

    def sum_for_others(m):
        def one(t, carry):
            j = jnp.where(odd == 1, n_expert - 1 - t, t)

            @pl.when(summed_here(j))
            def _():
                await_slots(m, j)

                @pl.when(m == 0)
                def _():
                    pick_arrival(j).wait_recv()

                @pl.when(m >= 2)
                def _():
                    term_copy(m - 2, j).wait_send()

                pick = asked_v[j, m]

                def combine(i, inner):
                    cols = columns_of(i)
                    sums_v[lax.rem(m, 2), j, :, cols] = picked(m, j, pick, cols).astype(
                        jnp.bfloat16
                    )
                    return inner

                lax.fori_loop(0, tiles, combine, 0, unroll=True)
                term_copy(m, j).start()

            return carry

        lax.fori_loop(0, n_expert, one, 0)

    offset = lax.broadcasted_iota(jnp.int32, (PACK, 2 * PACK), 1) - 2 * lax.broadcasted_iota(
        jnp.int32, (PACK, 2 * PACK), 0
    )

    def relay(m, q):
        part = pl.ds(pl.multiple_of(q * PACK, PACK), PACK)
        return pltpu.make_async_remote_copy(
            src_ref=out_v.at[m, part],
            dst_ref=inc_v.at[m, part],
            send_sem=relay_send.at[m, q],
            recv_sem=relay_recv.at[m, q],
            device_id={"pipe": jnp.maximum(pipe - 1, 0)},
            device_id_type=MESH,
        )

    def block(m):
        await_slots(m, expert)
        pick = pick_v[pair, m]

        def combine(i, inner):
            cols = columns_of(i)
            both = picked(m, expert, pick, cols)
            total_v[:, cols] = both[:rows] + both[rows:]
            return inner

        lax.fori_loop(0, tiles, combine, 0, unroll=True)

        def join(p, carry):
            @pl.when(p != pair)
            def _():
                term_arrival(m, p).wait_recv()

                def add(i, inner):
                    cols = columns_of(i)
                    total_v[:, cols] += terms_v[m, p, :, cols].astype(jnp.float32)
                    return inner

                lax.fori_loop(0, tiles, add, 0, unroll=True)

            return carry

        lax.fori_loop(0, n_pairs, join, 0)

        def step(q, inner):
            part = pl.ds(pl.multiple_of(q * PACK, PACK), PACK)

            @pl.when(pipe < n_pipe - 1)
            def _():
                relay(m, q).wait_recv()

            cross = lax.dot_general(
                inc_v[m, part],
                saved_v[m, pl.ds(pl.multiple_of(q * 2 * PACK, 2 * PACK), 2 * PACK)],
                (((1,), (1,)), ((), ())),
                preferred_element_type=jnp.float32,
            )
            probs = probs_v[m, part]
            weighted = jnp.zeros((PACK, experts), jnp.float32)
            for k in range(2):
                dot = jnp.sum(jnp.where(offset == k, cross, 0.0), axis=1, keepdims=True)
                weighted += dot * probs * chosen_v[m, k, part]
            dense = (weighted - probs * jnp.sum(weighted, axis=1, keepdims=True)).astype(jnp.bfloat16)
            dense_v[part] = dense

            def finish(i, innermost):
                cols = pl.ds(pl.multiple_of(i * tile, tile), tile)
                term = jnp.dot(dense, weight_v[:, cols], preferred_element_type=jnp.float32)
                whole = inc_v[m, part, cols].astype(jnp.float32) + total_v[part, cols] + term
                out_v[m, part, cols] = whole.astype(jnp.bfloat16)
                return innermost

            lax.fori_loop(0, width // tile, finish, 0, unroll=True)

            @pl.when(pipe > 0)
            def _():
                relay(m, q).start()

            out_copy(m, q).start()
            return inner

        lax.fori_loop(0, rows // PACK, step, 0)
        dense = dense_v[...]

        def weigh(i, inner):
            cols = pl.ds(pl.multiple_of(i * chunk, chunk), chunk)
            wpart_v[i] += lax.dot_general(
                dense,
                normed_v[m, :, cols],
                (((0,), (0,)), ((), ())),
                preferred_element_type=jnp.float32,
            )
            return inner

        lax.fori_loop(0, chunks, weigh, 0, unroll=8)

    def turn(m, carry):
        @pl.when(m < micro)
        def _():
            sum_for_others(m)

        @pl.when(m > 0)
        def _():
            block(m - 1)

        return carry

    lax.fori_loop(0, micro + 1, turn, 0)

    def part_copy(distance):
        other, place = member(distance)
        return pltpu.make_async_remote_copy(
            src_ref=wpart_v.at[jnp.minimum(other, chunks - 1)],
            dst_ref=wrecv_v.at[me],
            send_sem=part_send.at[other],
            recv_sem=part_recv.at[me],
            device_id=place,
            device_id_type=MESH,
        ), other

    def part_arrival(distance):
        other, place = member(distance)
        return pltpu.make_async_remote_copy(
            src_ref=wpart_v.at[0],
            dst_ref=wrecv_v.at[other],
            send_sem=part_send.at[other],
            recv_sem=part_recv.at[other],
            device_id=place,
            device_id_type=MESH,
        )

    def sum_copy(distance):
        other, place = member(distance)
        spot = jnp.minimum(me, chunks - 1)
        return pltpu.make_async_remote_copy(
            src_ref=wgrad_ref.at[spot],
            dst_ref=wgrad_ref.at[spot],
            send_sem=sum_send.at[other],
            recv_sem=sum_recv.at[me],
            device_id=place,
            device_id_type=MESH,
        )

    def sum_arrival(distance):
        other, place = member(distance)
        spot = jnp.minimum(other, chunks - 1)
        return pltpu.make_async_remote_copy(
            src_ref=wgrad_ref.at[spot],
            dst_ref=wgrad_ref.at[spot],
            send_sem=sum_send.at[other],
            recv_sem=sum_recv.at[other],
            device_id=place,
            device_id_type=MESH,
        ), other

    for distance in range(1, group):
        copy, other = part_copy(distance)

        @pl.when(other < chunks)
        def _():
            copy.start()

    @pl.when(me < chunks)
    def _():
        total = wpart_v[me]
        for distance in range(1, group):
            part_arrival(distance).wait_recv()
            total += wrecv_v[member(distance)[0]]
        wgrad_ref[me] = total * (1.0 / micro)
        for distance in range(1, group):
            sum_copy(distance).start()

    for distance in range(1, group):
        copy, other = sum_arrival(distance)

        @pl.when(other < chunks)
        def _():
            copy.wait_recv()

    for j in range(n_expert):

        @pl.when((expert != j) & jnp.logical_not(summed_here(j)))
        def _():
            if rest:
                tail_copy(j).wait_send()
            if whole_rows:
                for m in range(micro):
                    main_copy(m, j).wait_send()

        @pl.when(summed_here(j))
        def _():
            for m in range(max(micro - 2, 0), micro):
                term_copy(m, j).wait_send()

    for m in range(micro):
        for q in range(rows // PACK):
            out_copy(m, q).wait()

    for p in range(n_pairs):

        @pl.when(p != pair)
        def _():
            pick_copy(p).wait_send()

    @pl.when(pipe > 0)
    def _():
        for m in range(micro):
            for q in range(rows // PACK):
                relay(m, q).wait_send()

    for distance in range(1, group):
        copy, other = part_copy(distance)

        @pl.when(other < chunks)
        def _():
            copy.wait_send()

    @pl.when(me < chunks)
    def _():
        for distance in range(1, group):
            sum_copy(distance).wait_send()


def settle(out_ref, wgrad_ref, out_to, wgrad_to, sems):
    micro = out_ref.shape[0]
    copies = [pltpu.make_async_copy(wgrad_ref, wgrad_to, sems.at[sems.shape[0] - 1])]
    pieces = out_ref.shape[1] // PACK
    for i in range(micro * pieces):
        part = pl.ds(i % pieces * PACK, PACK)
        copies.append(
            pltpu.make_async_copy(
                out_ref.at[i // pieces, part], out_to.at[i // pieces, part], sems.at[i]
            )
        )
    for copy in copies:
        copy.start()
    for copy in copies:
        copy.wait()


def on_device(sizes, normed, saved_out, expert_grads, routes, router_weight, upstream):
    n_pipe, n_expert, n_dp = sizes
    micro, rows, width = normed.shape[1:]
    experts = router_weight.shape[2]
    capacity = expert_grads.shape[5]
    whole_rows = capacity // PACK * PACK
    rest = capacity - whole_rows
    tail_rows = -(-max(rest * micro, 1) // PACK) * PACK
    group = n_expert * n_dp
    chunks = min(group, width // 128)
    chunk = width // chunks
    grads = jnp.swapaxes(expert_grads.reshape(micro, n_expert, capacity, width), 1, 2)
    columns = 2 * (whole_rows + (tail_rows if rest else 0))
    main_shape = (
        (micro, n_expert, whole_rows, width) if whole_rows else (1, 1, PACK, width)
    )
    tail_shape = (n_expert, tail_rows, width) if rest else (1, tail_rows, width)
    n_pairs = n_expert // 2
    any_space = pl.BlockSpec(memory_space=pl.ANY)
    vmem = pl.BlockSpec(memory_space=pltpu.VMEM)
    dma = pltpu.SemaphoreType.DMA
    out, wgrad = pl.pallas_call(
        functools.partial(kernel, sizes),
        out_shape=(
            jax.ShapeDtypeStruct((micro, rows, width), jnp.bfloat16),
            jax.ShapeDtypeStruct((chunks, experts, chunk), jnp.float32),
        ),
        in_specs=[any_space] * 6,
        out_specs=(any_space, vmem),
        scratch_shapes=[
            pltpu.VMEM((micro, 2, rows), jnp.int32),
            pltpu.VMEM((experts, width), jnp.bfloat16),
            pltpu.VMEM((micro, capacity, n_expert, width), jnp.bfloat16),
            pltpu.VMEM(main_shape, jnp.bfloat16),
            pltpu.VMEM(tail_shape, jnp.bfloat16),
            pltpu.VMEM(main_shape, jnp.bfloat16),
            pltpu.VMEM(tail_shape, jnp.bfloat16),
            pltpu.VMEM((2, n_expert, rows, width), jnp.bfloat16),
            pltpu.VMEM((micro, n_pairs, rows, width), jnp.bfloat16),
            pltpu.VMEM((micro, rows, width), jnp.bfloat16),
            pltpu.VMEM((micro, rows, 2, width), jnp.bfloat16),
            pltpu.VMEM((micro, 2 * rows, width), jnp.bfloat16),
            pltpu.VMEM((micro, rows, width), jnp.bfloat16),
            pltpu.VMEM((micro, rows, width), jnp.bfloat16),
            pltpu.VMEM((rows, width), jnp.float32),
            pltpu.VMEM((rows, experts), jnp.bfloat16),
            pltpu.VMEM((n_pairs, micro, 2 * rows, columns), jnp.bfloat16),
            pltpu.VMEM((n_expert, micro, rows, columns), jnp.bfloat16),
            pltpu.VMEM((micro, rows, experts), jnp.float32),
            pltpu.VMEM((micro, 2, rows, experts), jnp.float32),
            pltpu.VMEM((chunks, experts, chunk), jnp.float32),
            pltpu.VMEM((group, experts, chunk), jnp.float32),
            dma((micro,)),
            dma((micro, n_expert)),
            dma((micro, n_expert)),
            dma((n_expert,)),
            dma((n_expert,)),
            dma((n_pairs,)),
            dma((n_expert,)),
            dma((micro, n_expert)),
            dma((micro, n_pairs)),
            dma((4,)),
            dma,
            dma((micro, rows // PACK)),
            dma((micro, rows // PACK)),
            dma((micro, rows // PACK)),
            dma((group,)),
            dma((group,)),
            dma((group,)),
            dma((group,)),
        ],
        compiler_params=pltpu.CompilerParams(
            collective_id=0, has_side_effects=True, vmem_limit_bytes=60 * 2**20
        ),
        name="relay",
    )(
        grads,
        normed[0],
        saved_out[0],
        upstream,
        jnp.swapaxes(routes[0], 1, 2),
        router_weight[0].T,
    )
    out, wgrad = pl.pallas_call(
        settle,
        out_shape=(
            jax.ShapeDtypeStruct(out.shape, out.dtype),
            jax.ShapeDtypeStruct(wgrad.shape, wgrad.dtype),
        ),
        in_specs=[any_space] * 2,
        out_specs=(any_space, any_space),
        scratch_shapes=[dma((micro * (rows // PACK) + 1,))],
        compiler_params=pltpu.CompilerParams(vmem_limit_bytes=60 * 2**20),
        name="settle",
    )(out, wgrad)
    router_grad = jnp.transpose(wgrad, (0, 2, 1)).reshape(width, experts)
    return (out[None], router_grad[None])


def solution(mesh):
    in_specs = (
        P("pipe", None, ("expert", "dp"), None),
        P("pipe", None, ("expert", "dp"), None, None),
        P("pipe", None, "dp", "expert", None, None, None),
        P("pipe", None, ("expert", "dp"), None),
        P("pipe", None, None),
        P(None, ("expert", "dp"), None),
    )
    out_specs = (P("pipe", None, ("expert", "dp"), None), P("pipe", None, None))
    sizes = (mesh.shape["pipe"], mesh.shape["expert"], mesh.shape["dp"])
    return jax.shard_map(
        functools.partial(on_device, sizes),
        mesh=mesh,
        in_specs=in_specs,
        out_specs=out_specs,
        check_vma=False,
    )
```

```python
import functools

import jax
import jax.numpy as jnp
from jax import lax
from jax.experimental import pallas as pl
from jax.experimental.pallas import tpu as pltpu
from jax.sharding import PartitionSpec as P

MESH = pl.DeviceIdType.MESH
PACK = 16


def kernel(
    sizes,
    grads_ref,
    normed_ref,
    saved_ref,
    upstream_ref,
    routes_ref,
    weight_ref,
    out_ref,
    wgrad_ref,
    routes_v,
    weight_v,
    grads_v,
    main_v,
    tail_v,
    mate_main_v,
    mate_tail_v,
    sums_v,
    terms_v,
    normed_v,
    pairs_v,
    saved_v,
    inc_v,
    out_v,
    total_v,
    dense_v,
    pick_v,
    asked_v,
    probs_v,
    chosen_v,
    wpart_v,
    wrecv_v,
    grads_sem,
    main_send,
    main_recv,
    tail_send,
    tail_recv,
    pick_send,
    pick_recv,
    term_send,
    term_recv,
    load_sem,
    top_sem,
    relay_send,
    relay_recv,
    out_sem,
    part_send,
    part_recv,
    sum_send,
    sum_recv,
):
    n_pipe, n_expert, n_dp = sizes
    micro, rows, width = normed_v.shape
    experts = weight_ref.shape[0]
    capacity = grads_ref.shape[1]
    whole_rows = capacity // PACK * PACK
    rest = capacity - whole_rows
    tail_rows = tail_v.shape[1]
    columns = pick_v.shape[3]
    n_pairs = n_expert // 2
    group = n_expert * n_dp
    chunks, _, chunk = wpart_v.shape
    tile = min(width, 512)
    pipe = lax.axis_index("pipe")
    expert = lax.axis_index("expert")
    dp = lax.axis_index("dp")
    me = expert * n_dp + dp
    pair = expert // 2
    odd = lax.rem(expert, 2)
    mate = expert + 1 - 2 * odd

    def summed_here(j):
        return ((odd == 1) & (j > expert)) | ((odd == 0) & (j < expert))

    def member(distance):
        other = lax.rem(me + distance, group)
        return other, {"expert": other // n_dp, "dp": lax.rem(other, n_dp)}

    barrier = pltpu.get_barrier_semaphore()
    for distance in range(1, group):
        _, place = member(distance)
        pl.semaphore_signal(barrier, inc=1, device_id=place, device_id_type=MESH)

    @pl.when(pipe > 0)
    def _():
        pl.semaphore_signal(barrier, inc=1, device_id={"pipe": pipe - 1}, device_id_type=MESH)

    @pl.when(pipe < n_pipe - 1)
    def _():
        pl.semaphore_signal(barrier, inc=1, device_id={"pipe": pipe + 1}, device_id_type=MESH)

    def grads_load(m):
        return pltpu.make_async_copy(grads_ref.at[m], grads_v.at[m], grads_sem.at[m])

    grads_load(0).start()
    loads = [
        pltpu.make_async_copy(normed_ref, normed_v, load_sem.at[0]),
        pltpu.make_async_copy(saved_ref, pairs_v, load_sem.at[1]),
        pltpu.make_async_copy(routes_ref, routes_v, load_sem.at[2]),
        pltpu.make_async_copy(weight_ref, weight_v, load_sem.at[3]),
    ]
    top_load = pltpu.make_async_copy(upstream_ref, inc_v, top_sem)
    def tail_copy(j):
        return pltpu.make_async_remote_copy(
            src_ref=tail_v.at[j],
            dst_ref=mate_tail_v.at[j],
            send_sem=tail_send.at[j],
            recv_sem=tail_recv.at[j],
            device_id={"expert": mate},
            device_id_type=MESH,
        )

    def main_copy(m, j):
        return pltpu.make_async_remote_copy(
            src_ref=main_v.at[m, j],
            dst_ref=mate_main_v.at[m, j],
            send_sem=main_send.at[m, j],
            recv_sem=main_recv.at[m, j],
            device_id={"expert": mate},
            device_id_type=MESH,
        )

    def first_of(p):
        return jnp.where(p == pair, expert, jnp.where(p < pair, 2 * p + 1, 2 * p))

    def pick_copy(p):
        return pltpu.make_async_remote_copy(
            src_ref=pick_v.at[p, :, pl.ds(0, rows)],
            dst_ref=asked_v.at[expert],
            send_sem=pick_send.at[p],
            recv_sem=pick_recv.at[expert],
            device_id={"expert": first_of(p)},
            device_id_type=MESH,
        )

    def pick_arrival(j):
        return pltpu.make_async_remote_copy(
            src_ref=pick_v.at[0, :, pl.ds(0, rows)],
            dst_ref=asked_v.at[j],
            send_sem=pick_send.at[0],
            recv_sem=pick_recv.at[j],
            device_id={"expert": j},
            device_id_type=MESH,
        )

    def term_copy(m, j):
        return pltpu.make_async_remote_copy(
            src_ref=sums_v.at[lax.rem(m, 2), j],
            dst_ref=terms_v.at[m, pair],
            send_sem=term_send.at[m, j],
            recv_sem=term_recv.at[m, pair],
            device_id={"expert": j},
            device_id_type=MESH,
        )

    def term_arrival(m, p):
        return pltpu.make_async_remote_copy(
            src_ref=sums_v.at[0, 0],
            dst_ref=terms_v.at[m, p],
            send_sem=term_send.at[m, 0],
            recv_sem=term_recv.at[m, p],
            device_id={"expert": first_of(p)},
            device_id_type=MESH,
        )

    def far(t):
        j = jnp.where(odd == 1, t, n_expert - 1 - t)
        return j, (j != expert) & (j != mate) & jnp.logical_not(summed_here(j))

    tiles = width // tile

    def columns_of(i):
        return pl.ds(pl.multiple_of(i * tile, tile), tile)

    if rest:
        shape = (n_expert * tail_rows, micro * rest * n_expert)
        row, col = (lax.broadcasted_iota(jnp.int32, shape, axis) for axis in (0, 1))
        tail_order = (
            col == lax.rem(row, tail_rows) * n_expert + lax.div(row, tail_rows)
        ).astype(jnp.bfloat16)
    if whole_rows:
        shape = (n_expert * whole_rows, n_expert * whole_rows)
        row, col = (lax.broadcasted_iota(jnp.int32, shape, axis) for axis in (0, 1))
        main_order = (
            col == lax.rem(row, whole_rows) * n_expert + lax.div(row, whole_rows)
        ).astype(jnp.bfloat16)

    def regroup_tail(i, carry):
        cols = columns_of(i)
        slots = jnp.concatenate(
            [
                grads_v[m, whole_rows:, :, cols].reshape(rest * n_expert, tile)
                for m in range(micro)
            ],
            axis=0,
        )
        ordered = jnp.dot(tail_order, slots, preferred_element_type=jnp.float32)
        tail_v[:, :, cols] = ordered.astype(jnp.bfloat16).reshape(n_expert, tail_rows, tile)
        return carry

    def regroup_main(m):
        def regroup(i, carry):
            cols = columns_of(i)
            slots = grads_v[m, :whole_rows, :, cols].reshape(whole_rows * n_expert, tile)
            ordered = jnp.dot(main_order, slots, preferred_element_type=jnp.float32)
            main_v[m, :, :, cols] = ordered.astype(jnp.bfloat16).reshape(
                n_expert, whole_rows, tile
            )
            return carry

        lax.fori_loop(0, tiles, regroup, 0, unroll=4)

    def send_first(t):
        j, send = far(t)

        @pl.when(send)
        def _():
            main_copy(0, j).start()

    def send_first_tail(t):
        j, send = far(t)

        @pl.when(send)
        def _():
            tail_copy(j).start()

    grads_load(0).wait()
    for m in range(1, micro):
        grads_load(m).start()
    for load in loads:
        load.start()

    @pl.when(pipe == n_pipe - 1)
    def _():
        top_load.start()

    if whole_rows:
        regroup_main(0)
    pl.semaphore_wait(
        barrier,
        group - 1 + jnp.where(pipe > 0, 1, 0) + jnp.where(pipe < n_pipe - 1, 1, 0),
    )
    if whole_rows:
        send_first(0)
    for m in range(1, micro):
        grads_load(m).wait()
    if rest:
        lax.fori_loop(0, tiles, regroup_tail, 0, unroll=4)
        send_first_tail(0)

    wpart_v[...] = jnp.zeros_like(wpart_v)
    for load in loads:
        load.wait()

    weight = weight_v[...]
    earlier = (
        lax.broadcasted_iota(jnp.int32, (rows, rows), 0)
        > lax.broadcasted_iota(jnp.int32, (rows, rows), 1)
    ).astype(jnp.bfloat16)
    same = lax.broadcasted_iota(jnp.int32, (rows, rows), 0) == lax.broadcasted_iota(
        jnp.int32, (rows, rows), 1
    )
    expert_ids = lax.broadcasted_iota(jnp.int32, (rows, experts), 1)

    def regroup(i, carry):
        m, cols = i // (width // tile), pl.ds(pl.multiple_of(lax.rem(i, width // tile) * tile, tile), tile)
        saved_v[m, :, cols] = pairs_v[m, :, :, cols].reshape(2 * rows, tile)
        return carry

    def route(m, carry):
        logits = lax.dot_general(
            normed_v[m], weight, (((1,), (1,)), ((), ())), preferred_element_type=jnp.float32
        )
        expl = jnp.exp(logits)
        probs = expl / jnp.sum(expl, axis=-1, keepdims=True)
        probs_v[m] = probs
        named = [
            jnp.sum(jnp.where(same, routes_v[m, k : k + 1, :], 0), axis=1, keepdims=True)
            for k in range(2)
        ]
        first = (named[0] == expert_ids).astype(jnp.float32)
        second = (named[1] == expert_ids).astype(jnp.float32)
        chosen_v[m, 0] = first
        chosen_v[m, 1] = second
        either = first + second
        before = jnp.dot(earlier, either.astype(jnp.bfloat16), preferred_element_type=jnp.float32)
        slot = jnp.where(either > 0.5, before.astype(jnp.int32), -1)
        ids = lax.broadcasted_iota(jnp.int32, (rows, columns), 1)
        for p in range(n_pairs):
            first_expert = first_of(p)
            pick = jnp.zeros((rows, columns), jnp.float32)
            for place, e in enumerate((first_expert, 4 * p + 1 - first_expert)):
                this = expert_ids == e
                at = jnp.sum(jnp.where(this, slot, 0), axis=1, keepdims=True)
                gate = jnp.sum(jnp.where(this, probs, 0.0), axis=1, keepdims=True)
                late = 2 * whole_rows + place * tail_rows + at - whole_rows + m * rest
                there = jnp.where(at < whole_rows, at + place * whole_rows, late)
                there = jnp.where(at < 0, -1, there)
                pick += jnp.where(there == ids, gate, 0.0)
            high = pick.astype(jnp.bfloat16)
            low = (pick - high.astype(jnp.float32)).astype(jnp.bfloat16)
            pick_v[p, m, pl.ds(0, rows)] = high
            pick_v[p, m, pl.ds(rows, rows)] = low
        return carry

    lax.fori_loop(0, micro, route, 0)
    for p in range(n_pairs):

        @pl.when(p != pair)
        def _():
            pick_copy(p).start()

    for t in range(1, n_expert):
        if whole_rows:
            send_first(t)
        if rest:
            send_first_tail(t)

    def send_near(m):
        if rest and m == 0:
            tail_copy(mate).start()
        if whole_rows:
            main_copy(m, mate).start()

    for m in range(1, micro):
        if whole_rows:
            regroup_main(m)
            for t in range(n_expert):
                j, send = far(t)

                @pl.when(send)
                def _():
                    main_copy(m, j).start()

        send_near(m - 1)
    send_near(micro - 1)

    lax.fori_loop(0, micro * (width // tile), regroup, 0)

    @pl.when(pipe == n_pipe - 1)
    def _():
        top_load.wait()

    def out_copy(m, q):
        part = pl.ds(pl.multiple_of(q * PACK, PACK), PACK)
        return pltpu.make_async_copy(
            out_v.at[m, part], out_ref.at[m, part], out_sem.at[m, q]
        )

    def await_slots(m, j):
        if whole_rows:
            main_copy(m, j).wait_recv()
        if rest:

            @pl.when(m == 0)
            def _():
                tail_copy(j).wait_recv()

    def picked(m, j, pick, cols):
        slots = []
        if whole_rows:
            slots += [main_v[m, j, :, cols], mate_main_v[m, j, :, cols]]
        if rest:
            slots += [tail_v[j, :, cols], mate_tail_v[j, :, cols]]
        return jnp.dot(
            pick, jnp.concatenate(slots, axis=0), preferred_element_type=jnp.float32
        )

    def sum_for_others(m):
        def one(t, carry):
            j = jnp.where(odd == 1, n_expert - 1 - t, t)

            @pl.when(summed_here(j))
            def _():
                await_slots(m, j)

                @pl.when(m == 0)
                def _():
                    pick_arrival(j).wait_recv()

                @pl.when(m >= 2)
                def _():
                    term_copy(m - 2, j).wait_send()

                pick = asked_v[j, m]

                def combine(i, inner):
                    cols = columns_of(i)
                    sums_v[lax.rem(m, 2), j, :, cols] = picked(m, j, pick, cols).astype(
                        jnp.bfloat16
                    )
                    return inner

                lax.fori_loop(0, tiles, combine, 0, unroll=True)
                term_copy(m, j).start()

            return carry

        lax.fori_loop(0, n_expert, one, 0)

    offset = lax.broadcasted_iota(jnp.int32, (PACK, 2 * PACK), 1) - 2 * lax.broadcasted_iota(
        jnp.int32, (PACK, 2 * PACK), 0
    )

    def relay(m, q):
        part = pl.ds(pl.multiple_of(q * PACK, PACK), PACK)
        return pltpu.make_async_remote_copy(
            src_ref=out_v.at[m, part],
            dst_ref=inc_v.at[m, part],
            send_sem=relay_send.at[m, q],
            recv_sem=relay_recv.at[m, q],
            device_id={"pipe": jnp.maximum(pipe - 1, 0)},
            device_id_type=MESH,
        )

    def block(m):
        await_slots(m, expert)
        pick = pick_v[pair, m]

        def combine(i, inner):
            cols = columns_of(i)
            both = picked(m, expert, pick, cols)
            total_v[:, cols] = both[:rows] + both[rows:]
            return inner

        lax.fori_loop(0, tiles, combine, 0, unroll=True)

        def join(p, carry):
            @pl.when(p != pair)
            def _():
                term_arrival(m, p).wait_recv()

                def add(i, inner):
                    cols = columns_of(i)
                    total_v[:, cols] += terms_v[m, p, :, cols].astype(jnp.float32)
                    return inner

                lax.fori_loop(0, tiles, add, 0, unroll=True)

            return carry

        lax.fori_loop(0, n_pairs, join, 0)

        def step(q, inner):
            part = pl.ds(pl.multiple_of(q * PACK, PACK), PACK)

            @pl.when(pipe < n_pipe - 1)
            def _():
                relay(m, q).wait_recv()

            cross = lax.dot_general(
                inc_v[m, part],
                saved_v[m, pl.ds(pl.multiple_of(q * 2 * PACK, 2 * PACK), 2 * PACK)],
                (((1,), (1,)), ((), ())),
                preferred_element_type=jnp.float32,
            )
            probs = probs_v[m, part]
            weighted = jnp.zeros((PACK, experts), jnp.float32)
            for k in range(2):
                dot = jnp.sum(jnp.where(offset == k, cross, 0.0), axis=1, keepdims=True)
                weighted += dot * probs * chosen_v[m, k, part]
            dense = (weighted - probs * jnp.sum(weighted, axis=1, keepdims=True)).astype(jnp.bfloat16)
            dense_v[part] = dense

            def finish(i, innermost):
                cols = pl.ds(pl.multiple_of(i * tile, tile), tile)
                term = jnp.dot(dense, weight_v[:, cols], preferred_element_type=jnp.float32)
                whole = inc_v[m, part, cols].astype(jnp.float32) + total_v[part, cols] + term
                out_v[m, part, cols] = whole.astype(jnp.bfloat16)
                return innermost

            lax.fori_loop(0, width // tile, finish, 0, unroll=True)

            @pl.when(pipe > 0)
            def _():
                relay(m, q).start()

            out_copy(m, q).start()
            return inner

        lax.fori_loop(0, rows // PACK, step, 0)
        dense = dense_v[...]

        def weigh(i, inner):
            cols = pl.ds(pl.multiple_of(i * chunk, chunk), chunk)
            wpart_v[i] += lax.dot_general(
                dense,
                normed_v[m, :, cols],
                (((0,), (0,)), ((), ())),
                preferred_element_type=jnp.float32,
            )
            return inner

        lax.fori_loop(0, chunks, weigh, 0, unroll=8)

    def turn(m, carry):
        @pl.when(m < micro)
        def _():
            sum_for_others(m)

        @pl.when(m > 0)
        def _():
            block(m - 1)

        return carry

    lax.fori_loop(0, micro + 1, turn, 0)

    def part_copy(distance):
        other, place = member(distance)
        return pltpu.make_async_remote_copy(
            src_ref=wpart_v.at[jnp.minimum(other, chunks - 1)],
            dst_ref=wrecv_v.at[me],
            send_sem=part_send.at[other],
            recv_sem=part_recv.at[me],
            device_id=place,
            device_id_type=MESH,
        ), other

    def part_arrival(distance):
        other, place = member(distance)
        return pltpu.make_async_remote_copy(
            src_ref=wpart_v.at[0],
            dst_ref=wrecv_v.at[other],
            send_sem=part_send.at[other],
            recv_sem=part_recv.at[other],
            device_id=place,
            device_id_type=MESH,
        )

    def sum_copy(distance):
        other, place = member(distance)
        spot = jnp.minimum(me, chunks - 1)
        return pltpu.make_async_remote_copy(
            src_ref=wgrad_ref.at[spot],
            dst_ref=wgrad_ref.at[spot],
            send_sem=sum_send.at[other],
            recv_sem=sum_recv.at[me],
            device_id=place,
            device_id_type=MESH,
        )

    def sum_arrival(distance):
        other, place = member(distance)
        spot = jnp.minimum(other, chunks - 1)
        return pltpu.make_async_remote_copy(
            src_ref=wgrad_ref.at[spot],
            dst_ref=wgrad_ref.at[spot],
            send_sem=sum_send.at[other],
            recv_sem=sum_recv.at[other],
            device_id=place,
            device_id_type=MESH,
        ), other

    for distance in range(1, group):
        copy, other = part_copy(distance)

        @pl.when(other < chunks)
        def _():
            copy.start()

    @pl.when(me < chunks)
    def _():
        total = wpart_v[me]
        for distance in range(1, group):
            part_arrival(distance).wait_recv()
            total += wrecv_v[member(distance)[0]]
        wgrad_ref[me] = total * (1.0 / micro)
        for distance in range(1, group):
            sum_copy(distance).start()

    for distance in range(1, group):
        copy, other = sum_arrival(distance)

        @pl.when(other < chunks)
        def _():
            copy.wait_recv()

    for j in range(n_expert):

        @pl.when((expert != j) & jnp.logical_not(summed_here(j)))
        def _():
            if rest:
                tail_copy(j).wait_send()
            if whole_rows:
                for m in range(micro):
                    main_copy(m, j).wait_send()

        @pl.when(summed_here(j))
        def _():
            for m in range(max(micro - 2, 0), micro):
                term_copy(m, j).wait_send()

    for m in range(micro):
        for q in range(rows // PACK):
            out_copy(m, q).wait()

    for p in range(n_pairs):

        @pl.when(p != pair)
        def _():
            pick_copy(p).wait_send()

    @pl.when(pipe > 0)
    def _():
        for m in range(micro):
            for q in range(rows // PACK):
                relay(m, q).wait_send()

    for distance in range(1, group):
        copy, other = part_copy(distance)

        @pl.when(other < chunks)
        def _():
            copy.wait_send()

    @pl.when(me < chunks)
    def _():
        for distance in range(1, group):
            sum_copy(distance).wait_send()


def settle(out_ref, wgrad_ref, out_to, wgrad_to, out_v, wgrad_v, load_sems, store_sems):
    micro = out_ref.shape[0]
    ways = [(wgrad_ref, wgrad_v, wgrad_to)]
    for m in range(micro):
        ways.append((out_ref.at[m], out_v.at[m], out_to.at[m]))
    loads, stores = [], []
    for i, (source, held, target) in enumerate(ways):
        loads.append(pltpu.make_async_copy(source, held, load_sems.at[i]))
        stores.append(pltpu.make_async_copy(held, target, store_sems.at[i]))
    for load in loads:
        load.start()
    for load, store in zip(loads, stores):
        load.wait()
        store.start()
    for store in stores:
        store.wait()


def on_device(sizes, normed, saved_out, expert_grads, routes, router_weight, upstream):
    n_pipe, n_expert, n_dp = sizes
    micro, rows, width = normed.shape[1:]
    experts = router_weight.shape[2]
    capacity = expert_grads.shape[5]
    whole_rows = capacity // PACK * PACK
    rest = capacity - whole_rows
    tail_rows = -(-max(rest * micro, 1) // PACK) * PACK
    group = n_expert * n_dp
    chunks = min(group, width // 128)
    chunk = width // chunks
    grads = jnp.swapaxes(expert_grads.reshape(micro, n_expert, capacity, width), 1, 2)
    columns = 2 * (whole_rows + (tail_rows if rest else 0))
    main_shape = (
        (micro, n_expert, whole_rows, width) if whole_rows else (1, 1, PACK, width)
    )
    tail_shape = (n_expert, tail_rows, width) if rest else (1, tail_rows, width)
    n_pairs = n_expert // 2
    any_space = pl.BlockSpec(memory_space=pl.ANY)
    vmem = pl.BlockSpec(memory_space=pltpu.VMEM)
    dma = pltpu.SemaphoreType.DMA
    out, wgrad = pl.pallas_call(
        functools.partial(kernel, sizes),
        out_shape=(
            jax.ShapeDtypeStruct((micro, rows, width), jnp.bfloat16),
            jax.ShapeDtypeStruct((chunks, experts, chunk), jnp.float32),
        ),
        in_specs=[any_space] * 6,
        out_specs=(any_space, vmem),
        scratch_shapes=[
            pltpu.VMEM((micro, 2, rows), jnp.int32),
            pltpu.VMEM((experts, width), jnp.bfloat16),
            pltpu.VMEM((micro, capacity, n_expert, width), jnp.bfloat16),
            pltpu.VMEM(main_shape, jnp.bfloat16),
            pltpu.VMEM(tail_shape, jnp.bfloat16),
            pltpu.VMEM(main_shape, jnp.bfloat16),
            pltpu.VMEM(tail_shape, jnp.bfloat16),
            pltpu.VMEM((2, n_expert, rows, width), jnp.bfloat16),
            pltpu.VMEM((micro, n_pairs, rows, width), jnp.bfloat16),
            pltpu.VMEM((micro, rows, width), jnp.bfloat16),
            pltpu.VMEM((micro, rows, 2, width), jnp.bfloat16),
            pltpu.VMEM((micro, 2 * rows, width), jnp.bfloat16),
            pltpu.VMEM((micro, rows, width), jnp.bfloat16),
            pltpu.VMEM((micro, rows, width), jnp.bfloat16),
            pltpu.VMEM((rows, width), jnp.float32),
            pltpu.VMEM((rows, experts), jnp.bfloat16),
            pltpu.VMEM((n_pairs, micro, 2 * rows, columns), jnp.bfloat16),
            pltpu.VMEM((n_expert, micro, rows, columns), jnp.bfloat16),
            pltpu.VMEM((micro, rows, experts), jnp.float32),
            pltpu.VMEM((micro, 2, rows, experts), jnp.float32),
            pltpu.VMEM((chunks, experts, chunk), jnp.float32),
            pltpu.VMEM((group, experts, chunk), jnp.float32),
            dma((micro,)),
            dma((micro, n_expert)),
            dma((micro, n_expert)),
            dma((n_expert,)),
            dma((n_expert,)),
            dma((n_pairs,)),
            dma((n_expert,)),
            dma((micro, n_expert)),
            dma((micro, n_pairs)),
            dma((4,)),
            dma,
            dma((micro, rows // PACK)),
            dma((micro, rows // PACK)),
            dma((micro, rows // PACK)),
            dma((group,)),
            dma((group,)),
            dma((group,)),
            dma((group,)),
        ],
        compiler_params=pltpu.CompilerParams(
            collective_id=0, has_side_effects=True, vmem_limit_bytes=60 * 2**20
        ),
        name="relay",
    )(
        grads,
        normed[0],
        saved_out[0],
        upstream,
        jnp.swapaxes(routes[0], 1, 2),
        router_weight[0].T,
    )
    out, wgrad = pl.pallas_call(
        settle,
        out_shape=(
            jax.ShapeDtypeStruct(out.shape, out.dtype),
            jax.ShapeDtypeStruct(wgrad.shape, wgrad.dtype),
        ),
        in_specs=[any_space] * 2,
        out_specs=(any_space, any_space),
        scratch_shapes=[
            pltpu.VMEM(out.shape, out.dtype),
            pltpu.VMEM(wgrad.shape, wgrad.dtype),
            dma((micro + 1,)),
            dma((micro + 1,)),
        ],
        compiler_params=pltpu.CompilerParams(vmem_limit_bytes=60 * 2**20),
        name="settle",
    )(out, wgrad)
    router_grad = jnp.transpose(wgrad, (0, 2, 1)).reshape(width, experts)
    return (out[None], router_grad[None])


def solution(mesh):
    in_specs = (
        P("pipe", None, ("expert", "dp"), None),
        P("pipe", None, ("expert", "dp"), None, None),
        P("pipe", None, "dp", "expert", None, None, None),
        P("pipe", None, ("expert", "dp"), None),
        P("pipe", None, None),
        P(None, ("expert", "dp"), None),
    )
    out_specs = (P("pipe", None, ("expert", "dp"), None), P("pipe", None, None))
    sizes = (mesh.shape["pipe"], mesh.shape["expert"], mesh.shape["dp"])
    return jax.shard_map(
        functools.partial(on_device, sizes),
        mesh=mesh,
        in_specs=in_specs,
        out_specs=out_specs,
        check_vma=False,
    )
```

```python
import functools

import jax
import jax.numpy as jnp
from jax import lax
from jax.experimental import pallas as pl
from jax.experimental.pallas import tpu as pltpu
from jax.sharding import PartitionSpec as P

MESH = pl.DeviceIdType.MESH
PACK = 16


def kernel(
    sizes,
    grads_ref,
    normed_ref,
    saved_ref,
    upstream_ref,
    routes_ref,
    weight_ref,
    out_ref,
    wgrad_ref,
    routes_v,
    weight_v,
    grads_v,
    main_v,
    tail_v,
    mate_main_v,
    mate_tail_v,
    sums_v,
    terms_v,
    normed_v,
    pairs_v,
    saved_v,
    inc_v,
    out_v,
    total_v,
    dense_v,
    pick_v,
    asked_v,
    probs_v,
    chosen_v,
    wpart_v,
    wrecv_v,
    grads_sem,
    main_send,
    main_recv,
    tail_send,
    tail_recv,
    pick_send,
    pick_recv,
    term_send,
    term_recv,
    load_sem,
    top_sem,
    relay_send,
    relay_recv,
    out_sem,
    part_send,
    part_recv,
    sum_send,
    sum_recv,
):
    n_pipe, n_expert, n_dp = sizes
    micro, rows, width = normed_v.shape
    experts = weight_ref.shape[0]
    capacity = grads_ref.shape[1]
    whole_rows = capacity // PACK * PACK
    rest = capacity - whole_rows
    tail_rows = tail_v.shape[1]
    columns = pick_v.shape[3]
    n_pairs = n_expert // 2
    group = n_expert * n_dp
    chunks, _, chunk = wpart_v.shape
    tile = min(width, 512)
    pipe = lax.axis_index("pipe")
    expert = lax.axis_index("expert")
    dp = lax.axis_index("dp")
    me = expert * n_dp + dp
    pair = expert // 2
    odd = lax.rem(expert, 2)
    mate = expert + 1 - 2 * odd

    def summed_here(j):
        return ((odd == 1) & (j > expert)) | ((odd == 0) & (j < expert))

    def member(distance):
        other = lax.rem(me + distance, group)
        return other, {"expert": other // n_dp, "dp": lax.rem(other, n_dp)}

    barrier = pltpu.get_barrier_semaphore()
    for distance in range(1, group):
        _, place = member(distance)
        pl.semaphore_signal(barrier, inc=1, device_id=place, device_id_type=MESH)

    @pl.when(pipe > 0)
    def _():
        pl.semaphore_signal(barrier, inc=1, device_id={"pipe": pipe - 1}, device_id_type=MESH)

    @pl.when(pipe < n_pipe - 1)
    def _():
        pl.semaphore_signal(barrier, inc=1, device_id={"pipe": pipe + 1}, device_id_type=MESH)

    def grads_load(m):
        return pltpu.make_async_copy(grads_ref.at[m], grads_v.at[m], grads_sem.at[m])

    grads_load(0).start()
    loads = [
        pltpu.make_async_copy(normed_ref, normed_v, load_sem.at[0]),
        pltpu.make_async_copy(saved_ref, pairs_v, load_sem.at[1]),
        pltpu.make_async_copy(routes_ref, routes_v, load_sem.at[2]),
        pltpu.make_async_copy(weight_ref, weight_v, load_sem.at[3]),
    ]
    top_load = pltpu.make_async_copy(upstream_ref, inc_v, top_sem)
    def tail_copy(j):
        return pltpu.make_async_remote_copy(
            src_ref=tail_v.at[j],
            dst_ref=mate_tail_v.at[j],
            send_sem=tail_send.at[j],
            recv_sem=tail_recv.at[j],
            device_id={"expert": mate},
            device_id_type=MESH,
        )

    def main_copy(m, j):
        return pltpu.make_async_remote_copy(
            src_ref=main_v.at[m, j],
            dst_ref=mate_main_v.at[m, j],
            send_sem=main_send.at[m, j],
            recv_sem=main_recv.at[m, j],
            device_id={"expert": mate},
            device_id_type=MESH,
        )

    def first_of(p):
        return jnp.where(p == pair, expert, jnp.where(p < pair, 2 * p + 1, 2 * p))

    def pick_copy(p):
        return pltpu.make_async_remote_copy(
            src_ref=pick_v.at[p, :, pl.ds(0, rows)],
            dst_ref=asked_v.at[expert],
            send_sem=pick_send.at[p],
            recv_sem=pick_recv.at[expert],
            device_id={"expert": first_of(p)},
            device_id_type=MESH,
        )

    def pick_arrival(j):
        return pltpu.make_async_remote_copy(
            src_ref=pick_v.at[0, :, pl.ds(0, rows)],
            dst_ref=asked_v.at[j],
            send_sem=pick_send.at[0],
            recv_sem=pick_recv.at[j],
            device_id={"expert": j},
            device_id_type=MESH,
        )

    def term_copy(m, j):
        return pltpu.make_async_remote_copy(
            src_ref=sums_v.at[lax.rem(m, 2), j],
            dst_ref=terms_v.at[m, pair],
            send_sem=term_send.at[m, j],
            recv_sem=term_recv.at[m, pair],
            device_id={"expert": j},
            device_id_type=MESH,
        )

    def term_arrival(m, p):
        return pltpu.make_async_remote_copy(
            src_ref=sums_v.at[0, 0],
            dst_ref=terms_v.at[m, p],
            send_sem=term_send.at[m, 0],
            recv_sem=term_recv.at[m, p],
            device_id={"expert": first_of(p)},
            device_id_type=MESH,
        )

    def far(t):
        j = jnp.where(odd == 1, t, n_expert - 1 - t)
        return j, (j != expert) & (j != mate) & jnp.logical_not(summed_here(j))

    tiles = width // tile

    def columns_of(i):
        return pl.ds(pl.multiple_of(i * tile, tile), tile)

    if rest:
        shape = (n_expert * tail_rows, micro * rest * n_expert)
        row, col = (lax.broadcasted_iota(jnp.int32, shape, axis) for axis in (0, 1))
        tail_order = (
            col == lax.rem(row, tail_rows) * n_expert + lax.div(row, tail_rows)
        ).astype(jnp.bfloat16)
    if whole_rows:
        shape = (n_expert * whole_rows, n_expert * whole_rows)
        row, col = (lax.broadcasted_iota(jnp.int32, shape, axis) for axis in (0, 1))
        main_order = (
            col == lax.rem(row, whole_rows) * n_expert + lax.div(row, whole_rows)
        ).astype(jnp.bfloat16)

    def regroup_tail(i, carry):
        cols = columns_of(i)
        slots = jnp.concatenate(
            [
                grads_v[m, whole_rows:, :, cols].reshape(rest * n_expert, tile)
                for m in range(micro)
            ],
            axis=0,
        )
        ordered = jnp.dot(tail_order, slots, preferred_element_type=jnp.float32)
        tail_v[:, :, cols] = ordered.astype(jnp.bfloat16).reshape(n_expert, tail_rows, tile)
        return carry

    def regroup_main(m):
        def regroup(i, carry):
            cols = columns_of(i)
            slots = grads_v[m, :whole_rows, :, cols].reshape(whole_rows * n_expert, tile)
            ordered = jnp.dot(main_order, slots, preferred_element_type=jnp.float32)
            main_v[m, :, :, cols] = ordered.astype(jnp.bfloat16).reshape(
                n_expert, whole_rows, tile
            )
            return carry

        lax.fori_loop(0, tiles, regroup, 0, unroll=4)

    def send_first(t):
        j, send = far(t)

        @pl.when(send)
        def _():
            main_copy(0, j).start()

    def send_first_tail(t):
        j, send = far(t)

        @pl.when(send)
        def _():
            tail_copy(j).start()

    grads_load(0).wait()
    for m in range(1, micro):
        grads_load(m).start()
    for load in loads:
        load.start()

    @pl.when(pipe == n_pipe - 1)
    def _():
        top_load.start()

    if whole_rows:
        regroup_main(0)
    pl.semaphore_wait(
        barrier,
        group - 1 + jnp.where(pipe > 0, 1, 0) + jnp.where(pipe < n_pipe - 1, 1, 0),
    )
    if whole_rows:
        send_first(0)
    for m in range(1, micro):
        grads_load(m).wait()
    if rest:
        lax.fori_loop(0, tiles, regroup_tail, 0, unroll=4)
        send_first_tail(0)

    wpart_v[...] = jnp.zeros_like(wpart_v)
    for load in loads:
        load.wait()

    weight = weight_v[...]
    earlier = (
        lax.broadcasted_iota(jnp.int32, (rows, rows), 0)
        > lax.broadcasted_iota(jnp.int32, (rows, rows), 1)
    ).astype(jnp.bfloat16)
    same = lax.broadcasted_iota(jnp.int32, (rows, rows), 0) == lax.broadcasted_iota(
        jnp.int32, (rows, rows), 1
    )
    expert_ids = lax.broadcasted_iota(jnp.int32, (rows, experts), 1)

    def regroup(i, carry):
        m, cols = i // (width // tile), pl.ds(pl.multiple_of(lax.rem(i, width // tile) * tile, tile), tile)
        saved_v[m, :, cols] = pairs_v[m, :, :, cols].reshape(2 * rows, tile)
        return carry

    def route(m, carry):
        logits = lax.dot_general(
            normed_v[m], weight, (((1,), (1,)), ((), ())), preferred_element_type=jnp.float32
        )
        expl = jnp.exp(logits)
        probs = expl / jnp.sum(expl, axis=-1, keepdims=True)
        probs_v[m] = probs
        named = [
            jnp.sum(jnp.where(same, routes_v[m, k : k + 1, :], 0), axis=1, keepdims=True)
            for k in range(2)
        ]
        first = (named[0] == expert_ids).astype(jnp.float32)
        second = (named[1] == expert_ids).astype(jnp.float32)
        chosen_v[m, 0] = first
        chosen_v[m, 1] = second
        either = first + second
        before = jnp.dot(earlier, either.astype(jnp.bfloat16), preferred_element_type=jnp.float32)
        slot = jnp.where(either > 0.5, before.astype(jnp.int32), -1)
        ids = lax.broadcasted_iota(jnp.int32, (rows, columns), 1)
        for p in range(n_pairs):
            first_expert = first_of(p)
            pick = jnp.zeros((rows, columns), jnp.float32)
            for place, e in enumerate((first_expert, 4 * p + 1 - first_expert)):
                this = expert_ids == e
                at = jnp.sum(jnp.where(this, slot, 0), axis=1, keepdims=True)
                gate = jnp.sum(jnp.where(this, probs, 0.0), axis=1, keepdims=True)
                late = 2 * whole_rows + place * tail_rows + at - whole_rows + m * rest
                there = jnp.where(at < whole_rows, at + place * whole_rows, late)
                there = jnp.where(at < 0, -1, there)
                pick += jnp.where(there == ids, gate, 0.0)
            high = pick.astype(jnp.bfloat16)
            low = (pick - high.astype(jnp.float32)).astype(jnp.bfloat16)
            pick_v[p, m, pl.ds(0, rows)] = high
            pick_v[p, m, pl.ds(rows, rows)] = low
        return carry

    lax.fori_loop(0, micro, route, 0)
    for p in range(n_pairs):

        @pl.when(p != pair)
        def _():
            pick_copy(p).start()

    for t in range(1, n_expert):
        if whole_rows:
            send_first(t)
        if rest:
            send_first_tail(t)

    def send_near(m):
        if rest and m == 0:
            tail_copy(mate).start()
        if whole_rows:
            main_copy(m, mate).start()

    for m in range(1, micro):
        if whole_rows:
            regroup_main(m)
            for t in range(n_expert):
                j, send = far(t)

                @pl.when(send)
                def _():
                    main_copy(m, j).start()

        send_near(m - 1)
    send_near(micro - 1)

    lax.fori_loop(0, micro * (width // tile), regroup, 0)

    @pl.when(pipe == n_pipe - 1)
    def _():
        top_load.wait()

    def out_copy(m, q):
        part = pl.ds(pl.multiple_of(q * PACK, PACK), PACK)
        return pltpu.make_async_copy(
            out_v.at[m, part], out_ref.at[m, part], out_sem.at[m, q]
        )

    def await_slots(m, j):
        if whole_rows:
            main_copy(m, j).wait_recv()
        if rest:

            @pl.when(m == 0)
            def _():
                tail_copy(j).wait_recv()

    def picked(m, j, pick, cols):
        slots = []
        if whole_rows:
            slots += [main_v[m, j, :, cols], mate_main_v[m, j, :, cols]]
        if rest:
            slots += [tail_v[j, :, cols], mate_tail_v[j, :, cols]]
        return jnp.dot(
            pick, jnp.concatenate(slots, axis=0), preferred_element_type=jnp.float32
        )

    def sum_for_others(m):
        def one(t, carry):
            j = jnp.where(odd == 1, n_expert - 1 - t, t)

            @pl.when(summed_here(j))
            def _():
                await_slots(m, j)

                @pl.when(m == 0)
                def _():
                    pick_arrival(j).wait_recv()

                @pl.when(m >= 2)
                def _():
                    term_copy(m - 2, j).wait_send()

                pick = asked_v[j, m]

                def combine(i, inner):
                    cols = columns_of(i)
                    sums_v[lax.rem(m, 2), j, :, cols] = picked(m, j, pick, cols).astype(
                        jnp.bfloat16
                    )
                    return inner

                lax.fori_loop(0, tiles, combine, 0, unroll=True)
                term_copy(m, j).start()

            return carry

        lax.fori_loop(0, n_expert, one, 0)

    offset = lax.broadcasted_iota(jnp.int32, (PACK, 2 * PACK), 1) - 2 * lax.broadcasted_iota(
        jnp.int32, (PACK, 2 * PACK), 0
    )

    def relay(m, q):
        part = pl.ds(pl.multiple_of(q * PACK, PACK), PACK)
        return pltpu.make_async_remote_copy(
            src_ref=out_v.at[m, part],
            dst_ref=inc_v.at[m, part],
            send_sem=relay_send.at[m, q],
            recv_sem=relay_recv.at[m, q],
            device_id={"pipe": jnp.maximum(pipe - 1, 0)},
            device_id_type=MESH,
        )

    def block(m):
        await_slots(m, expert)
        pick = pick_v[pair, m]

        def combine(i, inner):
            cols = columns_of(i)
            both = picked(m, expert, pick, cols)
            total_v[:, cols] = both[:rows] + both[rows:]
            return inner

        lax.fori_loop(0, tiles, combine, 0, unroll=True)

        def join(p, carry):
            @pl.when(p != pair)
            def _():
                term_arrival(m, p).wait_recv()

                def add(i, inner):
                    cols = columns_of(i)
                    total_v[:, cols] += terms_v[m, p, :, cols].astype(jnp.float32)
                    return inner

                lax.fori_loop(0, tiles, add, 0, unroll=True)

            return carry

        lax.fori_loop(0, n_pairs, join, 0)

        def step(q, inner):
            part = pl.ds(pl.multiple_of(q * PACK, PACK), PACK)

            @pl.when(pipe < n_pipe - 1)
            def _():
                relay(m, q).wait_recv()

            cross = lax.dot_general(
                inc_v[m, part],
                saved_v[m, pl.ds(pl.multiple_of(q * 2 * PACK, 2 * PACK), 2 * PACK)],
                (((1,), (1,)), ((), ())),
                preferred_element_type=jnp.float32,
            )
            probs = probs_v[m, part]
            weighted = jnp.zeros((PACK, experts), jnp.float32)
            for k in range(2):
                dot = jnp.sum(jnp.where(offset == k, cross, 0.0), axis=1, keepdims=True)
                weighted += dot * probs * chosen_v[m, k, part]
            dense = (weighted - probs * jnp.sum(weighted, axis=1, keepdims=True)).astype(jnp.bfloat16)
            dense_v[part] = dense

            def finish(i, innermost):
                cols = pl.ds(pl.multiple_of(i * tile, tile), tile)
                term = jnp.dot(dense, weight_v[:, cols], preferred_element_type=jnp.float32)
                whole = inc_v[m, part, cols].astype(jnp.float32) + total_v[part, cols] + term
                out_v[m, part, cols] = whole.astype(jnp.bfloat16)
                return innermost

            lax.fori_loop(0, width // tile, finish, 0, unroll=True)

            @pl.when(pipe > 0)
            def _():
                relay(m, q).start()

            out_copy(m, q).start()
            return inner

        lax.fori_loop(0, rows // PACK, step, 0, unroll=True)
        dense = dense_v[...]

        def weigh(i, inner):
            cols = pl.ds(pl.multiple_of(i * chunk, chunk), chunk)
            wpart_v[i] += lax.dot_general(
                dense,
                normed_v[m, :, cols],
                (((0,), (0,)), ((), ())),
                preferred_element_type=jnp.float32,
            )
            return inner

        lax.fori_loop(0, chunks, weigh, 0, unroll=8)

    def turn(m, carry):
        @pl.when(m < micro)
        def _():
            sum_for_others(m)

        @pl.when(m > 0)
        def _():
            block(m - 1)

        return carry

    lax.fori_loop(0, micro + 1, turn, 0)

    def part_copy(distance):
        other, place = member(distance)
        return pltpu.make_async_remote_copy(
            src_ref=wpart_v.at[jnp.minimum(other, chunks - 1)],
            dst_ref=wrecv_v.at[me],
            send_sem=part_send.at[other],
            recv_sem=part_recv.at[me],
            device_id=place,
            device_id_type=MESH,
        ), other

    def part_arrival(distance):
        other, place = member(distance)
        return pltpu.make_async_remote_copy(
            src_ref=wpart_v.at[0],
            dst_ref=wrecv_v.at[other],
            send_sem=part_send.at[other],
            recv_sem=part_recv.at[other],
            device_id=place,
            device_id_type=MESH,
        )

    def sum_copy(distance):
        other, place = member(distance)
        spot = jnp.minimum(me, chunks - 1)
        return pltpu.make_async_remote_copy(
            src_ref=wgrad_ref.at[spot],
            dst_ref=wgrad_ref.at[spot],
            send_sem=sum_send.at[other],
            recv_sem=sum_recv.at[me],
            device_id=place,
            device_id_type=MESH,
        )

    def sum_arrival(distance):
        other, place = member(distance)
        spot = jnp.minimum(other, chunks - 1)
        return pltpu.make_async_remote_copy(
            src_ref=wgrad_ref.at[spot],
            dst_ref=wgrad_ref.at[spot],
            send_sem=sum_send.at[other],
            recv_sem=sum_recv.at[other],
            device_id=place,
            device_id_type=MESH,
        ), other

    for distance in range(1, group):
        copy, other = part_copy(distance)

        @pl.when(other < chunks)
        def _():
            copy.start()

    @pl.when(me < chunks)
    def _():
        total = wpart_v[me]
        for distance in range(1, group):
            part_arrival(distance).wait_recv()
            total += wrecv_v[member(distance)[0]]
        wgrad_ref[me] = total * (1.0 / micro)
        for distance in range(1, group):
            sum_copy(distance).start()

    for distance in range(1, group):
        copy, other = sum_arrival(distance)

        @pl.when(other < chunks)
        def _():
            copy.wait_recv()

    for j in range(n_expert):

        @pl.when((expert != j) & jnp.logical_not(summed_here(j)))
        def _():
            if rest:
                tail_copy(j).wait_send()
            if whole_rows:
                for m in range(micro):
                    main_copy(m, j).wait_send()

        @pl.when(summed_here(j))
        def _():
            for m in range(max(micro - 2, 0), micro):
                term_copy(m, j).wait_send()

    for m in range(micro):
        for q in range(rows // PACK):
            out_copy(m, q).wait()

    for p in range(n_pairs):

        @pl.when(p != pair)
        def _():
            pick_copy(p).wait_send()

    @pl.when(pipe > 0)
    def _():
        for m in range(micro):
            for q in range(rows // PACK):
                relay(m, q).wait_send()

    for distance in range(1, group):
        copy, other = part_copy(distance)

        @pl.when(other < chunks)
        def _():
            copy.wait_send()

    @pl.when(me < chunks)
    def _():
        for distance in range(1, group):
            sum_copy(distance).wait_send()


def settle(out_ref, wgrad_ref, out_to, wgrad_to, out_v, wgrad_v, load_sems, store_sems):
    micro = out_ref.shape[0]
    ways = [(wgrad_ref, wgrad_v, wgrad_to)]
    for m in range(micro):
        ways.append((out_ref.at[m], out_v.at[m], out_to.at[m]))
    loads, stores = [], []
    for i, (source, held, target) in enumerate(ways):
        loads.append(pltpu.make_async_copy(source, held, load_sems.at[i]))
        stores.append(pltpu.make_async_copy(held, target, store_sems.at[i]))
    for load in loads:
        load.start()
    for load, store in zip(loads, stores):
        load.wait()
        store.start()
    for store in stores:
        store.wait()


def on_device(sizes, normed, saved_out, expert_grads, routes, router_weight, upstream):
    n_pipe, n_expert, n_dp = sizes
    micro, rows, width = normed.shape[1:]
    experts = router_weight.shape[2]
    capacity = expert_grads.shape[5]
    whole_rows = capacity // PACK * PACK
    rest = capacity - whole_rows
    tail_rows = -(-max(rest * micro, 1) // PACK) * PACK
    group = n_expert * n_dp
    chunks = min(group, width // 128)
    chunk = width // chunks
    grads = jnp.swapaxes(expert_grads.reshape(micro, n_expert, capacity, width), 1, 2)
    columns = 2 * (whole_rows + (tail_rows if rest else 0))
    main_shape = (
        (micro, n_expert, whole_rows, width) if whole_rows else (1, 1, PACK, width)
    )
    tail_shape = (n_expert, tail_rows, width) if rest else (1, tail_rows, width)
    n_pairs = n_expert // 2
    any_space = pl.BlockSpec(memory_space=pl.ANY)
    vmem = pl.BlockSpec(memory_space=pltpu.VMEM)
    dma = pltpu.SemaphoreType.DMA
    out, wgrad = pl.pallas_call(
        functools.partial(kernel, sizes),
        out_shape=(
            jax.ShapeDtypeStruct((micro, rows, width), jnp.bfloat16),
            jax.ShapeDtypeStruct((chunks, experts, chunk), jnp.float32),
        ),
        in_specs=[any_space] * 6,
        out_specs=(any_space, vmem),
        scratch_shapes=[
            pltpu.VMEM((micro, 2, rows), jnp.int32),
            pltpu.VMEM((experts, width), jnp.bfloat16),
            pltpu.VMEM((micro, capacity, n_expert, width), jnp.bfloat16),
            pltpu.VMEM(main_shape, jnp.bfloat16),
            pltpu.VMEM(tail_shape, jnp.bfloat16),
            pltpu.VMEM(main_shape, jnp.bfloat16),
            pltpu.VMEM(tail_shape, jnp.bfloat16),
            pltpu.VMEM((2, n_expert, rows, width), jnp.bfloat16),
            pltpu.VMEM((micro, n_pairs, rows, width), jnp.bfloat16),
            pltpu.VMEM((micro, rows, width), jnp.bfloat16),
            pltpu.VMEM((micro, rows, 2, width), jnp.bfloat16),
            pltpu.VMEM((micro, 2 * rows, width), jnp.bfloat16),
            pltpu.VMEM((micro, rows, width), jnp.bfloat16),
            pltpu.VMEM((micro, rows, width), jnp.bfloat16),
            pltpu.VMEM((rows, width), jnp.float32),
            pltpu.VMEM((rows, experts), jnp.bfloat16),
            pltpu.VMEM((n_pairs, micro, 2 * rows, columns), jnp.bfloat16),
            pltpu.VMEM((n_expert, micro, rows, columns), jnp.bfloat16),
            pltpu.VMEM((micro, rows, experts), jnp.float32),
            pltpu.VMEM((micro, 2, rows, experts), jnp.float32),
            pltpu.VMEM((chunks, experts, chunk), jnp.float32),
            pltpu.VMEM((group, experts, chunk), jnp.float32),
            dma((micro,)),
            dma((micro, n_expert)),
            dma((micro, n_expert)),
            dma((n_expert,)),
            dma((n_expert,)),
            dma((n_pairs,)),
            dma((n_expert,)),
            dma((micro, n_expert)),
            dma((micro, n_pairs)),
            dma((4,)),
            dma,
            dma((micro, rows // PACK)),
            dma((micro, rows // PACK)),
            dma((micro, rows // PACK)),
            dma((group,)),
            dma((group,)),
            dma((group,)),
            dma((group,)),
        ],
        compiler_params=pltpu.CompilerParams(
            collective_id=0, has_side_effects=True, vmem_limit_bytes=60 * 2**20
        ),
        name="relay",
    )(
        grads,
        normed[0],
        saved_out[0],
        upstream,
        jnp.swapaxes(routes[0], 1, 2),
        router_weight[0].T,
    )
    out, wgrad = pl.pallas_call(
        settle,
        out_shape=(
            jax.ShapeDtypeStruct(out.shape, out.dtype),
            jax.ShapeDtypeStruct(wgrad.shape, wgrad.dtype),
        ),
        in_specs=[any_space] * 2,
        out_specs=(any_space, any_space),
        scratch_shapes=[
            pltpu.VMEM(out.shape, out.dtype),
            pltpu.VMEM(wgrad.shape, wgrad.dtype),
            dma((micro + 1,)),
            dma((micro + 1,)),
        ],
        compiler_params=pltpu.CompilerParams(vmem_limit_bytes=60 * 2**20),
        name="settle",
    )(out, wgrad)
    router_grad = jnp.transpose(wgrad, (0, 2, 1)).reshape(width, experts)
    return (out[None], router_grad[None])


def solution(mesh):
    in_specs = (
        P("pipe", None, ("expert", "dp"), None),
        P("pipe", None, ("expert", "dp"), None, None),
        P("pipe", None, "dp", "expert", None, None, None),
        P("pipe", None, ("expert", "dp"), None),
        P("pipe", None, None),
        P(None, ("expert", "dp"), None),
    )
    out_specs = (P("pipe", None, ("expert", "dp"), None), P("pipe", None, None))
    sizes = (mesh.shape["pipe"], mesh.shape["expert"], mesh.shape["dp"])
    return jax.shard_map(
        functools.partial(on_device, sizes),
        mesh=mesh,
        in_specs=in_specs,
        out_specs=out_specs,
        check_vma=False,
    )
```
